256 devices in a mesh: tm: 2 (over z_lo), row: 16 (over y, z_hi), col: 8 (over x, core).
Axes of the slice: x: 4, y: 4, z: 8 (z_hi: 4, z_lo: 2; z = z_hi * 2 + z_lo), core: 2. Of those that a mesh axis runs over, the one named last changes fastest.
Arguments:
- sweeps: bfloat16 [32, 16, 512, 1024], P(None, 'tm', 'row', 'col'), may hold values from -6 to 6
- temporal_kernel: bfloat16 [64, 32, 3, 3, 3], replicated, may hold values from -0.21875 to 0.21875
- temporal_bias: float32 [64], replicated, may hold values from -3 to 3
- frame_weights: float32 [16], replicated, may hold values from 0.02 to 0.3
- conv1_kernel: bfloat16 [128, 64, 3, 3], replicated, may hold values from -0.25 to 0.25
- conv1_bias: float32 [128], replicated, may hold values from -3 to 3
- conv2_kernel: bfloat16 [128, 128, 3, 3], replicated, may hold values from -0.1875 to 0.1875
- conv2_bias: float32 [128], replicated, may hold values from -3 to 3
Outputs:
- merged: bfloat16 [128, 512, 1024], P(None, ('row', 'tm'), 'col')
The draws below stay inside these ranges and needn't reach their ends.
All inputs are finite; a program needn't handle non-finite values.
Results may differ from the reference program's by a relative error of at most 0.015.
Values may be sent and summed in bfloat16 or wider, within the bound.
No kernel may reach another device: no remote copies, remote signals or barrier semaphores. Data moves between devices by JAX's collectives and lax.ppermute only.
A program may use at most 128 MiB of HBM per device.

```python
import jax
import jax.numpy as jnp
from jax import lax

HB = 32
CT = 64
CB = 128
RB = 32
FRAMES = 16
NR = 512
NC = 1024
N_ROW = 16


def steps_of(own_key, shape, cuts, low, high):
    factor_of, own = 1.0, jax.random.fold_in(own_key, 6)
    for position, shards_of in cuts:
        heights = jnp.exp(jax.random.uniform(jax.random.fold_in(own, position), (shards_of,), jnp.float32, low / len(cuts), high / len(cuts)))
        factor_of = factor_of * jnp.repeat(heights, shape[position] // shards_of).reshape([-1 if axis == position else 1 for axis in range(len(shape))])
    return factor_of


def scatter_about(own_key, dims, deviation, limit, split=(), held_as=jnp.bfloat16):
    loudness = steps_of(own_key, dims, split, -0.22, 0.18) if split else 1.0
    values = jax.random.normal(own_key, dims, jnp.float32) * deviation * loudness
    return jnp.minimum(jnp.maximum(values, -limit), limit).astype(held_as)


def setup_inputs(seed: int = 0) -> dict:
    streams_of = jax.random.split(jax.random.key(seed), 9)
    sweeps = scatter_about(streams_of[0], (HB, FRAMES, NR, NC), 1.0, 6.0, ((1, 2), (2, 16), (3, 8)))
    temporal_kernel = scatter_about(streams_of[1], (CT, HB, 3, 3, 3), (27 * HB) ** -0.5, 0.21875)
    temporal_bias = scatter_about(streams_of[2], (CT,), 0.5, 3.0, (), jnp.float32)
    frame_weights = jnp.clip(jax.random.uniform(streams_of[3], (FRAMES,), jnp.float32, 0.02, 0.3), 0.02, 0.3)
    conv1_kernel = scatter_about(streams_of[4], (CB, CT, 3, 3), (9 * CT) ** -0.5, 0.25)
    conv1_bias = scatter_about(streams_of[5], (CB,), 0.4, 3.0, (), jnp.float32)
    conv2_kernel = scatter_about(streams_of[6], (CB, CB, 3, 3), (9 * CB) ** -0.5, 0.1875)
    conv2_bias = scatter_about(streams_of[7], (CB,), 0.4, 3.0, (), jnp.float32)
    return {"sweeps": sweeps, "temporal_kernel": temporal_kernel, "temporal_bias": temporal_bias, "frame_weights": frame_weights, "conv1_kernel": conv1_kernel, "conv1_bias": conv1_bias, "conv2_kernel": conv2_kernel, "conv2_bias": conv2_bias}


def spatial(field, kernel, bias):
    out = lax.conv_general_dilated(field[None], kernel, (1, 1), ((1, 1), (1, 1)), dimension_numbers=("NCHW", "OIHW", "NCHW"), preferred_element_type=jnp.float32)[0]
    return jax.nn.relu(out + bias[:, None, None]).astype(jnp.bfloat16)


def reference(sweeps, temporal_kernel, temporal_bias, frame_weights, conv1_kernel, conv1_bias, conv2_kernel, conv2_bias):
    padded = jnp.pad(sweeps, ((0, 0), (0, 0), (1, 1), (0, 0)))

    def one_band(index):
        start = (index * RB).astype(jnp.int32)
        block = lax.dynamic_slice_in_dim(padded, start, RB + 2, 2)
        temporal = lax.conv_general_dilated(block[None], temporal_kernel, (1, 1, 1), ((1, 1), (0, 0), (1, 1)), dimension_numbers=("NCDHW", "OIDHW", "NCDHW"), preferred_element_type=jnp.float32)[0]
        temporal = jax.nn.relu(temporal + temporal_bias[:, None, None, None])
        return jnp.sum(temporal * frame_weights[None, :, None, None], axis=1).astype(jnp.bfloat16)

    bands = lax.map(one_band, jnp.arange(N_ROW, dtype=jnp.int32))
    collapsed = jnp.transpose(bands, (1, 0, 2, 3)).reshape(CT, NR, NC)
    hidden = spatial(collapsed, conv1_kernel, conv1_bias)
    return spatial(hidden, conv2_kernel, conv2_bias)
```

```python
import functools

import jax
import jax.numpy as jnp
from jax import lax
from jax.experimental import pallas as pl
from jax.experimental.pallas import tpu as pltpu
from jax.sharding import PartitionSpec as P

BF = jnp.bfloat16
F32 = jnp.float32
ANY = pl.BlockSpec(memory_space=pl.ANY)
VMEM = pl.BlockSpec(memory_space=pltpu.VMEM)
SMEM = pl.BlockSpec(memory_space=pltpu.SMEM)


def params():
    return pltpu.CompilerParams(vmem_limit_bytes=40 * 1024 * 1024)


def cost(flops, nbytes):
    return pl.CostEstimate(flops=int(flops), bytes_accessed=int(nbytes), transcendentals=0)


def struct(shape, dtype=BF):
    return jax.ShapeDtypeStruct(shape, dtype)


def dot(a, b):
    return jnp.dot(a, b, preferred_element_type=F32)


def lanes_of(shape):
    return lax.broadcasted_iota(jnp.int32, shape, len(shape) - 1)


def swap16():
    row = lax.broadcasted_iota(jnp.int32, (256, 256), 0)
    col = lax.broadcasted_iota(jnp.int32, (256, 256), 1)
    return jnp.where(col == (row % 16) * 16 + row // 16, 1.0, 0.0).astype(BF)


def pack_kernel(x, xt, up, dn, slab, sup, sdn, perm):
    frame = pl.program_id(0)

    @pl.when(frame == 0)
    def _():
        perm[...] = swap16()

    for cb in range(2):
        chans = slice(cb * 16, cb * 16 + 16)
        halves = [x[chans, 0, rb * 16 : rb * 16 + 16, :].reshape(256, 128) for rb in range(2)]
        y = dot(perm[...], jnp.concatenate(halves, axis=1)).astype(BF)
        for rb in range(2):
            xt[rb * 16 : rb * 16 + 16, chans, :] = y[:, rb * 128 : rb * 128 + 128].reshape(16, 16, 128)
    up[...] = xt[0:3]
    dn[...] = xt[29:32]

    @pl.when(frame == 7 - 7 * lax.axis_index("tm"))
    def _():
        slab[...] = xt[...]
        sup[...] = xt[0:3]
        sdn[...] = xt[29:32]


def pack(sweeps):
    frame_block = lambda rows: pl.BlockSpec((rows, 32, 128), lambda f: (0, f, 0))
    fixed_block = lambda rows: pl.BlockSpec((rows, 32, 128), lambda f: (0, 0, 0))
    return pl.pallas_call(
        pack_kernel,
        grid=(8,),
        in_specs=[pl.BlockSpec((32, 1, 32, 128), lambda f: (0, f, 0, 0))],
        out_specs=[frame_block(32), frame_block(3), frame_block(3), fixed_block(32), fixed_block(3), fixed_block(3)],
        out_shape=[
            struct((32, 256, 128)),
            struct((3, 256, 128)),
            struct((3, 256, 128)),
            struct((32, 32, 128)),
            struct((3, 32, 128)),
            struct((3, 32, 128)),
        ],
        scratch_shapes=[pltpu.VMEM((256, 256), BF)],
        compiler_params=params(),
        cost_estimate=cost(6e8, 4.6e6),
        name="pack",
    )(sweeps)


def weights_kernel(kt, k1, k2, b0, b1, b2, w, ws, w1, w2, c0, c1, c2):
    base = {}
    for d in range(3):
        for b in range(3):
            rows = [kt[a, b, d].astype(F32) for a in range(3)] + [jnp.zeros((32, 64), F32)]
            base[d, b] = jnp.concatenate(rows, axis=0).T
    shifted = {}
    for key, value in base.items():
        shifted[key + (0,)] = value.astype(BF)
        shifted[key + (1,)] = pltpu.roll(value, 32, 1).astype(BF)
    for d in range(3):
        for fo in range(2):
            for b in range(3):
                ws[fo * 64 : fo * 64 + 64, (b * 3 + d) * 128 : (b * 3 + d) * 128 + 128] = shifted[d, b, fo]
            for ro in range(2):
                top = d * 256 + fo * 128 + ro * 64
                for ri in range(4):
                    b = ri - ro
                    block = shifted[d, b, fo] if 0 <= b <= 2 else jnp.zeros((64, 128), BF)
                    w[top : top + 64, ri * 128 : ri * 128 + 128] = block
    w1[...] = k1[...].reshape(576, 128).astype(F32).T.astype(BF)
    w2[...] = k2[...].reshape(1152, 128).astype(F32).T.astype(BF)
    wide = jnp.concatenate([b0[...], jnp.zeros((1, 64), F32)], axis=1)
    c0[...] = jnp.broadcast_to(wide, (128, 128)).T[0:64]
    c1[...] = jnp.broadcast_to(b1[...], (128, 128)).T
    c2[...] = jnp.broadcast_to(b2[...], (128, 128)).T


def weights(kt, b0, k1, b1, k2, b2):
    return pl.pallas_call(
        weights_kernel,
        in_specs=[VMEM] * 6,
        out_specs=[VMEM] * 7,
        out_shape=[
            struct((768, 512)),
            struct((128, 1152)),
            struct((128, 576)),
            struct((128, 1152)),
            struct((64, 128), F32),
            struct((128, 128), F32),
            struct((128, 128), F32),
        ],
        compiler_params=params(),
        cost_estimate=cost(1e6, 3e6),
        name="weights",
    )(
        jnp.transpose(kt, (2, 3, 4, 1, 0)),
        jnp.transpose(k1, (2, 3, 1, 0)),
        jnp.transpose(k2, (2, 3, 1, 0)),
        b0.reshape(1, 64),
        b1.reshape(1, 128),
        b2.reshape(1, 128),
    )


def strip_pack_kernel(xt, up, dn, slab, sup, sdn, left, right):
    lane = lanes_of((16, 128))

    def gather(read, at):
        acc_l = jnp.zeros((16, 128), BF)
        acc_r = jnp.zeros((16, 128), BF)
        for row in range(38):
            here = (lane >= 3 * row) & (lane < 3 * row + 3)
            tile = read(row)
            acc_l = jnp.where(here, pltpu.roll(tile, 3 * row, 1), acc_l)
            acc_r = jnp.where(here, pltpu.roll(tile, 3 * row + 3, 1), acc_r)
        left[at, :] = acc_l
        right[at, :] = acc_r

    def source(above, middle, below, at):
        def read(row):
            if row < 3:
                return above[row, at, :]
            if row < 35:
                return middle[row - 3, at, :]
            return below[row - 35, at, :]

        return read

    @pl.loop(0, 16)
    def _(s):
        at = pl.ds(pl.multiple_of(s * 16, 16), 16)
        gather(source(up, xt, dn, at), at)

    for s in range(2):
        at = pl.ds(s * 16, 16)
        gather(source(sup, slab, sdn, at), pl.ds(256 + s * 16, 16))


def strip_pack(*args):
    return pl.pallas_call(
        strip_pack_kernel,
        in_specs=[VMEM] * 6,
        out_specs=[VMEM] * 2,
        out_shape=[struct((288, 128))] * 2,
        compiler_params=params(),
        cost_estimate=cost(1e8, 3e6),
        name="strip_pack",
    )(*args)


def temporal_kernel(own, xt, up, dn, slab, sup, sdn, w, bias, fw, *rest):
    if own:
        out, xs, sems = rest
        quads = 4
    else:
        out, shared, xs, sems = rest
        quads = 5
    t = lax.axis_index("tm")
    lower = t == 1 if own else t == 0
    depth = 4 * quads + 2
    first = jnp.where(lower, 38 - depth, 0)
    inner = depth - 3
    start = jnp.where(lower, 32 - inner, 0)
    at_slab = 288 * (1 - t)
    at_zero = pl.ds(pl.multiple_of(288 * t, 32), 32)
    at_slab = pl.ds(pl.multiple_of(at_slab, 32), 32)
    frames = pl.ds(32, 256)
    place = jnp.where(lower, 0, 3)

    def moves(edge, edge_slab, edge_at):
        return [
            pltpu.make_async_copy(xt.at[pl.ds(start, inner)], xs.at[pl.ds(place, inner), frames], sems.at[0]),
            pltpu.make_async_copy(slab.at[pl.ds(start, inner)], xs.at[pl.ds(place, inner), at_slab], sems.at[1]),
            pltpu.make_async_copy(edge, xs.at[pl.ds(edge_at, 3), frames], sems.at[2]),
            pltpu.make_async_copy(edge_slab, xs.at[pl.ds(edge_at, 3), at_slab], sems.at[3]),
        ]

    @pl.when(lower)
    def _():
        for move in moves(dn, sdn, inner):
            move.start()

    @pl.when(jnp.logical_not(lower))
    def _():
        for move in moves(up, sup, 0):
            move.start()

    xs[:, at_zero, :] = jnp.zeros((depth, 32, 128), BF)
    for move in moves(up, sup, 0):
        move.wait()

    wide_bias = jnp.concatenate([bias[...], bias[...]], axis=0)

    @pl.loop(0, quads)
    def _(n):
        base = 4 * n
        acc = [jnp.zeros((128, 128), F32) for _ in range(2)]
        for g in range(4):
            sub = slice(64 * g, 64 * g + 128)
            rhs = jnp.concatenate(
                [jnp.concatenate([xs[base + ri, sub, :], xs[base + 2 + ri, sub, :]], axis=1) for ri in range(4)],
                axis=0,
            )
            y = dot(w[...], rhs)
            for fo in range(2):
                scale = fw[t * 8 + 2 * g + fo]
                for half in range(2):
                    cols = slice(128 * half, 128 * half + 128)
                    part = [y[d * 256 + fo * 128 : d * 256 + fo * 128 + 128, cols] for d in range(3)]
                    z = part[1] + pltpu.roll(part[0], 1, 1) + pltpu.roll(part[2], 127, 1) + wide_bias
                    acc[half] = acc[half] + jnp.maximum(z, 0.0) * scale
        for half in range(2):
            for ro in range(2):
                out[base + 2 * half + ro] = acc[half][ro * 64 : ro * 64 + 64].astype(out.dtype)
        if not own:

            @pl.when(n == 4 * t)
            def _():
                for half in range(2):
                    for ro in range(2):
                        shared[2 * half + ro] = acc[half][ro * 64 : ro * 64 + 64]


def temporal(own, xt, up, dn, slab, sup, sdn, w, bias, fw):
    quads = 4 if own else 5
    if own:
        out_shape = [struct((16, 64, 128), F32)]
    else:
        out_shape = [struct((20, 64, 128)), struct((4, 64, 128), F32)]
    return pl.pallas_call(
        functools.partial(temporal_kernel, own),
        in_specs=[ANY] * 6 + [VMEM, VMEM, SMEM],
        out_specs=[VMEM] * len(out_shape),
        out_shape=out_shape,
        scratch_shapes=[pltpu.VMEM((4 * quads + 2, 320, 128), BF), pltpu.SemaphoreType.DMA((4,))],
        compiler_params=params(),
        cost_estimate=cost(quads * 4 * 768 * 512 * 256 * 2, 3e6),
        name="temporal_own" if own else "temporal_partner",
    )(xt, up, dn, slab, sup, sdn, w, bias, fw)


def strip_temporal_kernel(own_l, own_r, nb_l, nb_r, ws, bias, fw, out, send, windows):
    t = lax.axis_index("tm")
    lane = lanes_of((16, 128))
    third = lane % 3

    windows[:, pl.ds(pl.multiple_of(288 * t, 32), 32), :] = jnp.zeros((9, 32, 256), BF)

    def fill(s, at):
        src = pl.ds(pl.multiple_of(s * 16, 16), 16)
        dst = pl.ds(pl.multiple_of(at, 16), 16)
        ol, nl, orr, nr = own_l[src, :], nb_l[src, :], own_r[src, :], nb_r[src, :]
        for b in range(3):
            for d in range(3):
                lo = pltpu.roll(nl, (128 - (3 * b + d)) % 128, 1)
                if d > 0:
                    lo = jnp.where(third < 3 - d, lo, pltpu.roll(ol, (128 - (3 * b + d - 3)) % 128, 1))
                hi = pltpu.roll(nr, (128 - (3 * b + d - 2)) % 128, 1)
                if d < 2:
                    hi = jnp.where(third < 2 - d, pltpu.roll(orr, 128 - (3 * b + d + 1), 1), hi)
                windows[b * 3 + d, dst, 0:128] = lo
                windows[b * 3 + d, dst, 128:256] = hi

    @pl.loop(0, 18)
    def _(s):
        fill(s, jnp.where(s < 16, 32 + 16 * s, 288 * (1 - t) + (s - 16) * 16))

    wide_bias = jnp.concatenate([bias[...], bias[...]], axis=1)
    acc = jnp.zeros((64, 256), F32)
    for g in range(4):
        rhs = jnp.concatenate([windows[k, 64 * g : 64 * g + 128, :] for k in range(9)], axis=0)
        y = dot(ws[...], rhs)
        for fo in range(2):
            acc = acc + jnp.maximum(y[fo * 64 : fo * 64 + 64] + wide_bias, 0.0) * fw[t * 8 + 2 * g + fo]
    for side in range(2):
        out[side] = acc[:, side * 128 : side * 128 + 128]
        send[side] = acc[:, side * 128 : side * 128 + 128].astype(BF)


def strip_temporal(own_l, own_r, nb_l, nb_r, ws, bias, fw):
    return pl.pallas_call(
        strip_temporal_kernel,
        in_specs=[VMEM] * 6 + [SMEM],
        out_specs=[VMEM] * 2,
        out_shape=[struct((2, 64, 128), F32), struct((2, 64, 128))],
        scratch_shapes=[pltpu.VMEM((9, 320, 256), BF)],
        compiler_params=params(),
        cost_estimate=cost(4 * 128 * 1152 * 256 * 2, 1e6),
        name="strip_temporal",
    )(own_l, own_r, nb_l, nb_r, ws, bias, fw)


def spatial_kernel(grid_rows, main, shared, partner, strips, partner_strips, w1, b1, w2, b2, out, c3, h3, ms):
    t = lax.axis_index("tm")
    row = lax.axis_index("row")
    col = lax.axis_index("col")
    first_col = col == 0
    last_col = col == lax.axis_size("col") - 1
    top = row * 32 + t * 16
    lane = lanes_of((64, 128))
    depth = lane // 3
    third = lane % 3

    def in_grid(g):
        return (g >= 0) & (g < grid_rows)

    edges = []
    for side in range(2):
        total = strips[side] + partner_strips[side].astype(F32)
        total = pltpu.roll(total, (128 - 48 * t) % 128, 1)
        off = (third < 2) & first_col if side == 0 else (third > 0) & last_col
        keep = in_grid(top + depth - 2) & jnp.logical_not(off)
        edges.append(jnp.where(keep, total, 0.0))
    edges_b = [edge.astype(BF) for edge in edges]

    def insert(index, value):
        value = value + partner[index].astype(F32)
        value = jnp.where(lane == 0, pltpu.roll(edges[0], lax.rem(254 - 3 * index, 128), 1), value)
        value = jnp.where(lane == 127, pltpu.roll(edges[1], 127 - 3 * index, 1), value)
        value = jnp.where(in_grid(top + index - 2), value, 0.0).astype(BF)
        c3[index, 0:64] = jnp.where(
            lane == 0, pltpu.roll(edges_b[0], 127 - 3 * index, 1), pltpu.roll(value, 1, 1)
        )
        c3[index, 64:128] = value
        c3[index, 128:192] = jnp.where(
            lane == 127, pltpu.roll(edges_b[1], 126 - 3 * index, 1), pltpu.roll(value, 127, 1)
        )

    @pl.loop(0, 16)
    def _(i):
        insert(i + 4 * t, main[i])

    @pl.loop(0, 4)
    def _(i):
        insert(i + 16 * (1 - t), shared[i])

    wide_b1 = jnp.concatenate([b1[...], b1[...]], axis=1)
    wide_b2 = jnp.concatenate([b2[...], b2[...]], axis=1)

    rhs = jnp.concatenate(
        [
            jnp.concatenate([pltpu.roll(edges_b[side], (128 - 3 * b - d) % 128, 1) for side in range(2)], axis=1)
            for b in range(3)
            for d in range(3)
        ],
        axis=0,
    )
    y = jnp.maximum(dot(w1[...], rhs) + wide_b1, 0.0)
    lane2 = lanes_of((128, 128))
    kept = in_grid(top + lane2 // 3 - 1)
    hs_l = jnp.where(kept & jnp.logical_not(first_col), y[:, :128], 0.0).astype(BF)
    hs_r = jnp.where(kept & jnp.logical_not(last_col), y[:, 128:], 0.0).astype(BF)

    @pl.loop(0, 9)
    def _(i):
        h = 2 * i
        rhs = jnp.concatenate(
            [jnp.concatenate([c3[h + b], c3[h + 1 + b]], axis=1) for b in range(3)], axis=0
        )
        y = jnp.maximum(dot(w1[...], rhs) + wide_b1, 0.0)
        for half in range(2):
            at = h + half
            value = jnp.where(in_grid(top + at - 1), y[:, half * 128 : half * 128 + 128], 0.0).astype(BF)
            h3[at, 0:128] = jnp.where(
                lane2 == 0, pltpu.roll(hs_l, lax.rem(128 - 3 * at, 128), 1), pltpu.roll(value, 1, 1)
            )
            h3[at, 128:256] = value
            h3[at, 256:384] = jnp.where(
                lane2 == 127, pltpu.roll(hs_r, 127 - 3 * at, 1), pltpu.roll(value, 127, 1)
            )

    @pl.loop(0, 8)
    def _(i):
        r = 2 * i
        rhs = jnp.concatenate(
            [jnp.concatenate([h3[r + b], h3[r + 1 + b]], axis=1) for b in range(3)], axis=0
        )
        y = jnp.maximum(dot(w2[...], rhs) + wide_b2, 0.0).astype(BF)
        ms[r] = y[:, :128]
        ms[r + 1] = y[:, 128:]

    perm = swap16()
    for pair in range(4):
        halves = [ms[:, (2 * pair + k) * 16 : (2 * pair + k) * 16 + 16, :].reshape(256, 128) for k in range(2)]
        y = dot(perm, jnp.concatenate(halves, axis=1)).astype(BF)
        for k in range(2):
            q = (2 * pair + k) * 16
            out[q : q + 16] = y[:, k * 128 : k * 128 + 128].reshape(16, 16, 128)


def spatial(grid_rows, *args):
    return pl.pallas_call(
        functools.partial(spatial_kernel, grid_rows),
        in_specs=[VMEM] * 9,
        out_specs=VMEM,
        out_shape=struct((128, 16, 128)),
        scratch_shapes=[
            pltpu.VMEM((20, 192, 128), BF),
            pltpu.VMEM((18, 384, 128), BF),
            pltpu.VMEM((16, 128, 128), BF),
        ],
        compiler_params=params(),
        cost_estimate=cost(1.2e9, 3e6),
        name="spatial",
    )(*args)


def shards(sweeps, kt, b0, fw, k1, b1, k2, b2):
    rows = lax.axis_size("row")
    cols = lax.axis_size("col")
    both = [(0, 1), (1, 0)]
    down = [(i, i + 1) for i in range(rows - 1)]
    up_route = [(i + 1, i) for i in range(rows - 1)]
    cross_down = [(t * rows + i, (1 - t) * rows + i + 1) for t in range(2) for i in range(rows - 1)]
    cross_up = [(t * rows + i + 1, (1 - t) * rows + i) for t in range(2) for i in range(rows - 1)]

    xt, first_rows, last_rows, slab, slab_first, slab_last = pack(sweeps)
    w, ws, w1, w2, c0, c1, c2 = weights(kt, b0, k1, b1, k2, b2)
    up = lax.ppermute(last_rows, "row", down)
    dn = lax.ppermute(first_rows, "row", up_route)
    halo = lax.ppermute(slab, "tm", both)
    sup = lax.ppermute(slab_last, ("tm", "row"), cross_down)
    sdn = lax.ppermute(slab_first, ("tm", "row"), cross_up)
    field = (xt, up, dn, halo, sup, sdn)

    own_l, own_r = strip_pack(*field)
    nb_l = lax.ppermute(own_r, "col", [(i, i + 1) for i in range(cols - 1)])
    nb_r = lax.ppermute(own_l, "col", [(i + 1, i) for i in range(cols - 1)])

    for_partner, shared = temporal(False, *field, w, c0, fw)
    partner = lax.ppermute(for_partner, "tm", both)
    strips, strips_send = strip_temporal(own_l, own_r, nb_l, nb_r, ws, c0, fw)
    partner_strips = lax.ppermute(strips_send, "tm", both)
    (main,) = temporal(True, *field, w, c0, fw)
    return spatial(rows * 32, main, shared, partner, strips, partner_strips, w1, c1, w2, c2)


def solution(mesh):
    placed = (P(None, "tm", "row", "col"), P(), P(), P(), P(), P(), P(), P())
    return jax.shard_map(
        shards, mesh=mesh, in_specs=placed, out_specs=P(None, ("row", "tm"), "col"), check_vma=False
    )
```

```python
import functools

import jax
import jax.numpy as jnp
from jax import lax
from jax.experimental import pallas as pl
from jax.experimental.pallas import tpu as pltpu
from jax.sharding import PartitionSpec as P

BF = jnp.bfloat16
F32 = jnp.float32
VMEM = pl.BlockSpec(memory_space=pltpu.VMEM)


def params(mib=14):
    return pltpu.CompilerParams(vmem_limit_bytes=mib * 1024 * 1024)


def cost(flops, nbytes):
    return pl.CostEstimate(flops=int(flops), bytes_accessed=int(nbytes), transcendentals=0)


def struct(shape, dtype=BF):
    return jax.ShapeDtypeStruct(shape, dtype)


def dot(a, b):
    return jnp.dot(a, b, preferred_element_type=F32)


def lanes_of(shape):
    return lax.broadcasted_iota(jnp.int32, shape, len(shape) - 1)


def swap16():
    row = lax.broadcasted_iota(jnp.int32, (256, 256), 0)
    col = lax.broadcasted_iota(jnp.int32, (256, 256), 1)
    return jnp.where(col == (row % 16) * 16 + row // 16, 1.0, 0.0).astype(BF)


def pack_kernel(x, xt, e_rows, o_rows):
    even = lax.axis_index("row") % 2 == 0
    perm = swap16()
    xt[:, 0:32, :] = jnp.zeros((32, 32, 128), BF)
    xt[:, 288:320, :] = jnp.zeros((32, 32, 128), BF)
    for f in range(8):
        for cb in range(2):
            halves = [
                x[cb * 16 : cb * 16 + 16, f, rb * 16 : rb * 16 + 16, :].reshape(256, 128) for rb in range(2)
            ]
            y = dot(perm, jnp.concatenate(halves, axis=1)).astype(BF)
            at = 32 + 32 * f + 16 * cb
            for rb in range(2):
                xt[rb * 16 : rb * 16 + 16, at : at + 16, :] = y[:, rb * 128 : rb * 128 + 128].reshape(16, 16, 128)
    e_start = jnp.where(even, 29, 0)
    e_rows[...] = xt[pl.ds(e_start, 3), 32:288]
    o_rows[...] = xt[pl.ds(29 - e_start, 3), 32:288]


def pack(sweeps):
    return pl.pallas_call(
        pack_kernel,
        in_specs=[VMEM],
        out_specs=[VMEM] * 3,
        out_shape=[
            struct((32, 320, 128)),
            struct((3, 256, 128)),
            struct((3, 256, 128)),
        ],
        compiler_params=params(),
        cost_estimate=cost(6e9, 4.6e6),
        name="pack",
    )(sweeps)


def taps(kt):
    base = {}
    for d in range(3):
        for b in range(3):
            rows = [kt[a, b, d].astype(F32) for a in range(3)] + [jnp.zeros((32, 64), F32)]
            value = jnp.concatenate(rows, axis=0).T
            base[d, b, 0] = value
            base[d, b, 1] = pltpu.roll(value, 32, 1)
    return base


def fill_w(base, w):
    for d in range(3):
        for fo in range(2):
            for ro in range(2):
                top = d * 256 + fo * 128 + ro * 64
                for ri in range(4):
                    b = ri - ro
                    block = base[d, b, fo].astype(BF) if 0 <= b <= 2 else jnp.zeros((64, 128), BF)
                    w[top : top + 64, ri * 128 : ri * 128 + 128] = block


def column(ref):
    n = ref.shape[1]
    wide = ref[...]
    if n < 128:
        wide = jnp.concatenate([wide, jnp.zeros((1, 128 - n), F32)], axis=1)
    return jnp.broadcast_to(wide, (128, 128)).T[0:n]


def scales_of(fw):
    both = column(fw)
    return jnp.where(lax.axis_index("tm") == 0, both[0:8], both[8:16])


def put_strips(lane, row, tile, left, right):
    here = (lane >= 3 * row) & (lane < 3 * row + 3)
    left = jnp.where(here, pltpu.roll(tile, 3 * row, 1), left)
    right = jnp.where(here, pltpu.roll(tile, 3 * row + 3, 1), right)
    return left, right


def halo_kernel(e_rows, o_rows, out):
    at = pl.ds(pl.multiple_of(224 * (1 - lax.axis_index("tm")), 32), 32)
    out[0:3] = e_rows[:, at, :]
    out[3:6] = o_rows[:, at, :]


def halo(e_rows, o_rows):
    return pl.pallas_call(
        halo_kernel,
        in_specs=[VMEM] * 2,
        out_specs=VMEM,
        out_shape=struct((6, 32, 128)),
        compiler_params=params(),
        cost_estimate=cost(1e10, 1e5),
        name="halo",
    )(e_rows, o_rows)


def strip_pack_kernel(left0, right0, e_rows, o_rows, slab, corner, left, right, e_send, o_send, corner_out, edge):
    lane = lanes_of((16, 128))
    even = lax.axis_index("row") % 2 == 0
    even_col = lax.axis_index("col") % 2 == 0
    e_at = jnp.where(even, 3, 0)
    corner_out[...] = corner[...]
    for k, (source, at) in enumerate(((e_rows, e_at), (o_rows, 3 - e_at))):
        edge[pl.ds(at, 3), 0:256] = source[...]
        edge[pl.ds(at, 3), 256:288] = corner[3 * k : 3 * k + 3]

    def add_edges(at, pair):
        for k in range(6):
            pair = put_strips(lane, k if k < 3 else 32 + k, edge[k, at, :], *pair)
        first, last = pair
        left[at, :] = first
        right[at, :] = last
        e_send[at, :] = jnp.where(even_col, last, first)
        o_send[at, :] = jnp.where(even_col, first, last)

    for s in range(16):
        at = slice(s * 16, s * 16 + 16)
        add_edges(at, (left0[at, :], right0[at, :]))

    for s in range(2):
        at = slice(s * 16, s * 16 + 16)
        pair = jnp.zeros((16, 128), BF), jnp.zeros((16, 128), BF)
        for row in range(32):
            pair = put_strips(lane, row + 3, slab[row, at, :], *pair)
        add_edges(slice(256 + s * 16, 272 + s * 16), pair)


def strip_pack(*args):
    return pl.pallas_call(
        strip_pack_kernel,
        in_specs=[VMEM] * 6,
        out_specs=[VMEM] * 5,
        out_shape=[struct((288, 128))] * 4 + [struct((6, 32, 128))],
        scratch_shapes=[pltpu.VMEM((6, 288, 128), BF)],
        compiler_params=params(),
        cost_estimate=cost(1e8, 1e6),
        name="strip_pack",
    )(*args)


def unit(acc, w, wide_bias, read, scales):
    rows = [read(k) for k in range(6)]
    rhs = jnp.concatenate(
        [jnp.concatenate([rows[ri], rows[ri + 2]], axis=1) for ri in range(4)], axis=0
    )
    y = dot(w[...], rhs)
    acc = list(acc)
    for fo in range(2):
        for half in range(2):
            cols = slice(128 * half, 128 * half + 128)
            part = [y[d * 256 + fo * 128 : d * 256 + fo * 128 + 128, cols] for d in range(3)]
            z = part[1] + pltpu.roll(part[0], 1, 1) + pltpu.roll(part[2], 127, 1) + wide_bias
            acc[half] = acc[half] + jnp.maximum(z, 0.0) * scales[fo]
    return acc


def blank():
    return [jnp.zeros((128, 128), F32) for _ in range(2)]


def store_quad(ref, base, acc):
    for half in range(2):
        for ro in range(2):
            ref[base + 2 * half + ro] = acc[half][ro * 64 : ro * 64 + 64].astype(ref.dtype)


def load_quad(ref, base):
    return [
        jnp.concatenate([ref[base + 2 * half], ref[base + 2 * half + 1]], axis=0) for half in range(2)
    ]


def interior_kernel(quads, xt, kt, b0, fw, *refs):
    if quads[0] == 0:
        out, left, right, slab, w = refs
    else:
        previous, out, w = refs
        for k in range(4 * quads[0]):
            out[k] = previous[k]
    t = lax.axis_index("tm")
    bias = column(b0)
    wide_bias = jnp.concatenate([bias, bias], axis=0)
    scale = scales_of(fw)
    scale = jnp.where(t == 0, scale[0:6], scale[2:8])
    fill_w(taps(kt), w)

    @pl.loop(quads[0], quads[1])
    def _(n):
        base = 4 * n
        acc = blank()
        for k in range(3):
            at = pl.ds(pl.multiple_of(64 * (k + t), 64), 128)
            scales = [scale[2 * k + fo : 2 * k + fo + 1] for fo in range(2)]
            acc = unit(acc, w, wide_bias, lambda r: xt[base + 1 + r, at, :], scales)
        store_quad(out, base, acc)

    if quads[0] == 0:
        lane = lanes_of((16, 128))

        @pl.loop(0, 16)
        def _(s):
            at = pl.ds(pl.multiple_of(s * 16, 16), 16)
            source = pl.ds(pl.multiple_of(s * 16 + 32, 16), 16)
            pair = jnp.zeros((16, 128), BF), jnp.zeros((16, 128), BF)
            for row in range(32):
                pair = put_strips(lane, row + 3, xt[row, source, :], *pair)
            left[at, :], right[at, :] = pair

        slab[...] = xt[:, pl.ds(pl.multiple_of(256 - 224 * t, 32), 32), :]


def interior(quads, xt, kt, b0, fw, *previous):
    out_shape = [struct((4 * quads[1], 64, 128), F32)]
    if not previous:
        out_shape += [struct((256, 128)), struct((256, 128)), struct((32, 32, 128))]
    return pl.pallas_call(
        functools.partial(interior_kernel, quads),
        in_specs=[VMEM] * (4 + len(previous)),
        out_specs=[VMEM] * len(out_shape),
        out_shape=out_shape,
        scratch_shapes=[pltpu.VMEM((768, 512), BF)],
        compiler_params=params(),
        cost_estimate=cost(1e3, 1e3),
        name="interior_%d" % quads[0],
    )(xt, kt, b0, fw, *previous)


def slab_kernel(xt, inner, slab, kt, b0, fw, out, w):
    t = lax.axis_index("tm")
    bias = column(b0)
    wide_bias = jnp.concatenate([bias, bias], axis=0)
    base = {key: jnp.where(t == 1, pltpu.roll(value, 96, 1), value) for key, value in taps(kt).items()}
    fill_w(base, w)
    own_at = pl.ds(pl.multiple_of(192 - 160 * t, 32), 96)
    scale = scales_of(fw)
    scale = jnp.where(t == 0, scale[6:8], scale[0:2])
    scales = [scale[fo : fo + 1] for fo in range(2)]

    @pl.loop(0, 7)
    def _(n):
        base = 4 * n

        def read(r):
            return jnp.concatenate([xt[base + 1 + r, own_at, :], slab[base + 1 + r]], axis=0)

        store_quad(out, base, unit(load_quad(inner, base), w, wide_bias, read, scales))


def slab_pairs(xt, inner, slab, kt, b0, fw):
    return pl.pallas_call(
        slab_kernel,
        in_specs=[VMEM] * 6,
        out_specs=VMEM,
        out_shape=struct((28, 64, 128), F32),
        scratch_shapes=[pltpu.VMEM((768, 512), BF)],
        compiler_params=params(),
        cost_estimate=cost(7 * 768 * 512 * 256 * 2, 3e6),
        name="slab_pairs",
    )(xt, inner, slab, kt, b0, fw)


def edge_kernel(own, xt, inner, e_rows, o_rows, slab, corner, kt, b0, fw, out, edge, w):
    t = lax.axis_index("tm")
    low = t if own else 1 - t
    bias = column(b0)
    wide_bias = jnp.concatenate([bias, bias], axis=0)
    fill_w(taps(kt), w)

    at_slab = pl.ds(pl.multiple_of(288 * (1 - t), 32), 32)
    edge[:, pl.ds(pl.multiple_of(288 * t, 32), 32), :] = jnp.zeros((6, 32, 128), BF)
    edge[pl.ds(3 - 3 * low, 3), 32:288] = xt[pl.ds(29 * low, 3), 32:288]
    edge[pl.ds(3 - 3 * low, 3), at_slab] = slab[pl.ds(29 * low, 3)]
    from_e = (lax.axis_index("row") + low) % 2 == 1

    @pl.when(from_e)
    def _():
        edge[pl.ds(3 * low, 3), 32:288] = e_rows[...]
        edge[pl.ds(3 * low, 3), at_slab] = corner[0:3]

    @pl.when(jnp.logical_not(from_e))
    def _():
        edge[pl.ds(3 * low, 3), 32:288] = o_rows[...]
        edge[pl.ds(3 * low, 3), at_slab] = corner[3:6]

    acc = blank()
    scale = scales_of(fw)
    for g in range(4):
        scales = [scale[2 * g + fo : 2 * g + fo + 1] for fo in range(2)]
        acc = unit(acc, w, wide_bias, lambda r: edge[r, 64 * g : 64 * g + 128, :], scales)
    if own:
        store_quad(out, 0, acc)
    else:
        out[pl.ds(4 - 4 * low, 16)] = inner[pl.ds(12 * low, 16)].astype(BF)
        store_quad(out, 16 * low, acc)


def edge_quad(own, xt, inner, e_rows, o_rows, slab, corner, kt, b0, fw):
    return pl.pallas_call(
        functools.partial(edge_kernel, own),
        in_specs=[VMEM] * 9,
        out_specs=VMEM,
        out_shape=struct((4, 64, 128), F32) if own else struct((20, 64, 128)),
        scratch_shapes=[pltpu.VMEM((6, 320, 128), BF), pltpu.VMEM((768, 512), BF)],
        compiler_params=params(),
        cost_estimate=cost(1e10 if own else 1e6, 2e6),
        name="edge_own" if own else "edge_partner",
    )(xt, inner, e_rows, o_rows, slab, corner, kt, b0, fw)


def strip_temporal_kernel(own_l, own_r, e_col, o_col, kt, b0, fw, out, send, windows, ws):
    t = lax.axis_index("tm")
    even = lax.axis_index("col") % 2 == 0
    lane = lanes_of((16, 128))
    third = lane % 3
    bias = column(b0)
    for (d, b, fo), value in taps(kt).items():
        ws[fo * 64 : fo * 64 + 64, (b * 3 + d) * 128 : (b * 3 + d) * 128 + 128] = value.astype(BF)

    windows[:, pl.ds(pl.multiple_of(288 * t, 32), 32), :] = jnp.zeros((9, 32, 256), BF)

    def fill(s, at):
        src = slice(s * 16, s * 16 + 16)
        dst = pl.ds(at if isinstance(at, int) else pl.multiple_of(at, 16), 16)
        ol, orr, ne, no = own_l[src, :], own_r[src, :], e_col[src, :], o_col[src, :]
        nl, nr = jnp.where(even, no, ne), jnp.where(even, ne, no)
        for b in range(3):
            for d in range(3):
                lo = pltpu.roll(nl, (128 - (3 * b + d)) % 128, 1)
                if d > 0:
                    lo = jnp.where(third < 3 - d, lo, pltpu.roll(ol, (128 - (3 * b + d - 3)) % 128, 1))
                hi = pltpu.roll(nr, (128 - (3 * b + d - 2)) % 128, 1)
                if d < 2:
                    hi = jnp.where(third < 2 - d, pltpu.roll(orr, 128 - (3 * b + d + 1), 1), hi)
                windows[b * 3 + d, dst, 0:128] = lo
                windows[b * 3 + d, dst, 128:256] = hi

    for s in range(18):
        fill(s, 32 + 16 * s if s < 16 else 288 * (1 - t) + (s - 16) * 16)

    wide_bias = jnp.concatenate([bias, bias], axis=1)
    both = scales_of(fw)
    both = jnp.concatenate([both, both], axis=1)
    scale = [both[k : k + 1] for k in range(8)]
    acc = jnp.zeros((64, 256), F32)
    for g in range(4):
        rhs = jnp.concatenate([windows[k, 64 * g : 64 * g + 128, :] for k in range(9)], axis=0)
        y = dot(ws[...], rhs)
        for fo in range(2):
            acc = acc + jnp.maximum(y[fo * 64 : fo * 64 + 64] + wide_bias, 0.0) * scale[2 * g + fo]
    for side in range(2):
        out[side] = acc[:, side * 128 : side * 128 + 128]
        send[side] = acc[:, side * 128 : side * 128 + 128].astype(BF)


def strip_temporal(own_l, own_r, e_col, o_col, kt, b0, fw):
    return pl.pallas_call(
        strip_temporal_kernel,
        in_specs=[VMEM] * 7,
        out_specs=[VMEM] * 2,
        out_shape=[struct((2, 64, 128), F32), struct((2, 64, 128))],
        scratch_shapes=[pltpu.VMEM((9, 320, 256), BF), pltpu.VMEM((128, 1152), BF)],
        compiler_params=params(),
        cost_estimate=cost(1e10, 1e6),
        name="strip_temporal",
    )(own_l, own_r, e_col, o_col, kt, b0, fw)


def spatial_kernel(grid_rows, inner, near, partner, strips, partner_strips, k1, b1, k2, b2, out, own, c3, h3, ms, w2):
    t = lax.axis_index("tm")
    row = lax.axis_index("row")
    col = lax.axis_index("col")
    first_col = col == 0
    last_col = col == lax.axis_size("col") - 1
    top = row * 32 + t * 16
    lane = lanes_of((64, 128))
    depth = lane // 3
    third = lane % 3

    own[pl.ds(4 - 4 * t, 16)] = inner[pl.ds(12 * t, 16)]
    own[pl.ds(16 * t, 4)] = near[...]
    w1 = k1[...].reshape(576, 128).astype(F32).T.astype(BF)
    for k in range(9):
        w2[:, k * 128 : k * 128 + 128] = k2[k // 3, k % 3]

    def in_grid(g):
        return (g >= 0) & (g < grid_rows)

    edges = []
    for side in range(2):
        total = strips[side] + partner_strips[side].astype(F32)
        total = pltpu.roll(total, (128 - 48 * t) % 128, 1)
        off = (third < 2) & first_col if side == 0 else (third > 0) & last_col
        keep = in_grid(top + depth - 2) & jnp.logical_not(off)
        edges.append(jnp.where(keep, total, 0.0).astype(BF))

    for r in range(20):
        value = (own[r] + partner[r].astype(F32)).astype(BF)
        value = jnp.where(lane == 0, pltpu.roll(edges[0], (126 - 3 * r) % 128, 1), value)
        value = jnp.where(lane == 127, pltpu.roll(edges[1], 127 - 3 * r, 1), value)
        value = jnp.where(in_grid(top + r - 2), value, jnp.zeros_like(value))
        c3[r, 0:64] = jnp.where(lane == 0, pltpu.roll(edges[0], 127 - 3 * r, 1), pltpu.roll(value, 1, 1))
        c3[r, 64:128] = value
        c3[r, 128:192] = jnp.where(
            lane == 127, pltpu.roll(edges[1], 126 - 3 * r, 1), pltpu.roll(value, 127, 1)
        )

    bias1 = column(b1)
    bias2 = column(b2)
    wide_b1 = jnp.concatenate([bias1, bias1], axis=1)
    wide_b2 = jnp.concatenate([bias2, bias2], axis=1)

    rhs = jnp.concatenate(
        [
            jnp.concatenate([pltpu.roll(edges[side], (128 - 3 * b - d) % 128, 1) for side in range(2)], axis=1)
            for b in range(3)
            for d in range(3)
        ],
        axis=0,
    )
    y = jnp.maximum(dot(w1, rhs) + wide_b1, 0.0)
    lane2 = lanes_of((128, 128))
    kept = in_grid(top + lane2 // 3 - 1)
    hs_l = jnp.where(kept & jnp.logical_not(first_col), y[:, :128], 0.0).astype(BF)
    hs_r = jnp.where(kept & jnp.logical_not(last_col), y[:, 128:], 0.0).astype(BF)

    for h in range(0, 18, 2):
        rhs = jnp.concatenate(
            [jnp.concatenate([c3[h + b], c3[h + 1 + b]], axis=1) for b in range(3)], axis=0
        )
        y = jnp.maximum(dot(w1, rhs) + wide_b1, 0.0)
        for at in range(h, h + 2):
            value = y[:, (at - h) * 128 : (at - h) * 128 + 128].astype(BF)
            value = jnp.where(in_grid(top + at - 1), value, jnp.zeros_like(value))
            h3[at, 0:128] = jnp.where(
                lane2 == 0, pltpu.roll(hs_l, (128 - 3 * at) % 128, 1), pltpu.roll(value, 1, 1)
            )
            h3[at, 128:256] = value
            h3[at, 256:384] = jnp.where(
                lane2 == 127, pltpu.roll(hs_r, 127 - 3 * at, 1), pltpu.roll(value, 127, 1)
            )

    for r in range(0, 16, 2):
        rhs = jnp.concatenate(
            [jnp.concatenate([h3[r + b], h3[r + 1 + b]], axis=1) for b in range(3)], axis=0
        )
        y = jnp.maximum(dot(w2[...], rhs) + wide_b2, 0.0).astype(BF)
        ms[r] = y[:, :128]
        ms[r + 1] = y[:, 128:]

    perm = swap16()
    for pair in range(4):
        halves = [ms[:, (2 * pair + k) * 16 : (2 * pair + k) * 16 + 16, :].reshape(256, 128) for k in range(2)]
        y = dot(perm, jnp.concatenate(halves, axis=1)).astype(BF)
        for k in range(2):
            q = (2 * pair + k) * 16
            out[q : q + 16] = y[:, k * 128 : k * 128 + 128].reshape(16, 16, 128)


def spatial(grid_rows, *args):
    return pl.pallas_call(
        functools.partial(spatial_kernel, grid_rows),
        in_specs=[VMEM] * 9,
        out_specs=VMEM,
        out_shape=struct((128, 16, 128)),
        scratch_shapes=[
            pltpu.VMEM((20, 64, 128), F32),
            pltpu.VMEM((20, 192, 128), BF),
            pltpu.VMEM((18, 384, 128), BF),
            pltpu.VMEM((16, 128, 128), BF),
            pltpu.VMEM((128, 1152), BF),
        ],
        compiler_params=params(),
        cost_estimate=cost(1.2e9, 3e6),
        name="spatial",
    )(*args)


def swaps(count, odd):
    return [pair for i in range(odd, count - 1, 2) for pair in ((i, i + 1), (i + 1, i))]


def shards(sweeps, kt, b0, fw, k1, b1, k2, b2):
    rows = lax.axis_size("row")
    cols = lax.axis_size("col")
    both = [(0, 1), (1, 0)]
    kt = jnp.transpose(kt, (2, 3, 4, 1, 0))
    k1 = jnp.transpose(k1, (2, 3, 1, 0))
    k2 = jnp.transpose(k2, (2, 3, 0, 1))
    b0, fw, b1, b2 = (value.reshape(1, -1) for value in (b0, fw, b1, b2))

    xt, e_rows, o_rows = pack(sweeps)
    e_rows = lax.ppermute(e_rows, "row", swaps(rows, 0))
    o_rows = lax.ppermute(o_rows, "row", swaps(rows, 1))
    inner, left0, right0, slab = interior((0, 3), xt, kt, b0, fw)
    slab = lax.ppermute(slab, "tm", both)
    (inner,) = interior((3, 7), xt, kt, b0, fw, inner)

    corner = lax.ppermute(halo(e_rows, o_rows), "tm", both)
    inner = slab_pairs(xt, inner, slab, kt, b0, fw)
    left, right, e_col, o_col, corner = strip_pack(left0, right0, e_rows, o_rows, slab, corner)
    e_col = lax.ppermute(e_col, "col", swaps(cols, 0))
    o_col = lax.ppermute(o_col, "col", swaps(cols, 1))

    field = (xt, inner, e_rows, o_rows, slab, corner, kt, b0, fw)
    partner = lax.ppermute(edge_quad(False, *field), "tm", both)
    strips, strips_send = strip_temporal(left, right, e_col, o_col, kt, b0, fw)
    partner_strips = lax.ppermute(strips_send, "tm", both)
    near = edge_quad(True, *field)
    return spatial(rows * 32, inner, near, partner, strips, partner_strips, k1, b1, k2, b2)


def solution(mesh):
    placed = (P(None, "tm", "row", "col"), P(), P(), P(), P(), P(), P(), P())
    return jax.shard_map(
        shards, mesh=mesh, in_specs=placed, out_specs=P(None, ("row", "tm"), "col"), check_vma=False
    )
```

```python
import functools

import jax
import jax.numpy as jnp
from jax import lax
from jax.experimental import pallas as pl
from jax.experimental.pallas import tpu as pltpu
from jax.sharding import PartitionSpec as P

BF = jnp.bfloat16
F32 = jnp.float32
ANY = pl.BlockSpec(memory_space=pl.ANY)
VMEM = pl.BlockSpec(memory_space=pltpu.VMEM)


def params(mib=14):
    return pltpu.CompilerParams(vmem_limit_bytes=mib * 1024 * 1024)


def cost(flops, nbytes):
    return pl.CostEstimate(flops=int(flops), bytes_accessed=int(nbytes), transcendentals=0)


def struct(shape, dtype=BF):
    return jax.ShapeDtypeStruct(shape, dtype)


def dot(a, b):
    return jnp.dot(a, b, preferred_element_type=F32)


def lanes_of(shape):
    return lax.broadcasted_iota(jnp.int32, shape, len(shape) - 1)


def swap16():
    row = lax.broadcasted_iota(jnp.int32, (256, 256), 0)
    col = lax.broadcasted_iota(jnp.int32, (256, 256), 1)
    return jnp.where(col == (row % 16) * 16 + row // 16, 1.0, 0.0).astype(BF)


def pack_kernel(x, xt, e_rows, o_rows):
    even = lax.axis_index("row") % 2 == 0
    perm = swap16()
    xt[:, 0:32, :] = jnp.zeros((32, 32, 128), BF)
    xt[:, 288:320, :] = jnp.zeros((32, 32, 128), BF)
    for f in range(8):
        for cb in range(2):
            halves = [
                x[cb * 16 : cb * 16 + 16, f, rb * 16 : rb * 16 + 16, :].reshape(256, 128) for rb in range(2)
            ]
            y = dot(perm, jnp.concatenate(halves, axis=1)).astype(BF)
            at = 32 + 32 * f + 16 * cb
            for rb in range(2):
                xt[rb * 16 : rb * 16 + 16, at : at + 16, :] = y[:, rb * 128 : rb * 128 + 128].reshape(16, 16, 128)
    e_start = jnp.where(even, 29, 0)
    e_rows[...] = xt[pl.ds(e_start, 3), 32:288]
    o_rows[...] = xt[pl.ds(29 - e_start, 3), 32:288]


def pack(sweeps):
    return pl.pallas_call(
        pack_kernel,
        in_specs=[VMEM],
        out_specs=[VMEM] * 3,
        out_shape=[
            struct((32, 320, 128)),
            struct((3, 256, 128)),
            struct((3, 256, 128)),
        ],
        compiler_params=params(),
        cost_estimate=cost(6e9, 4.6e6),
        name="pack",
    )(sweeps)


def taps(kt):
    base = {}
    for d in range(3):
        for b in range(3):
            rows = [kt[a, b, d].astype(F32) for a in range(3)] + [jnp.zeros((32, 64), F32)]
            value = jnp.concatenate(rows, axis=0).T
            base[d, b, 0] = value
            base[d, b, 1] = pltpu.roll(value, 32, 1)
    return base


def fill_w(base, w):
    for d in range(3):
        for fo in range(2):
            for ro in range(2):
                top = d * 256 + fo * 128 + ro * 64
                for ri in range(4):
                    b = ri - ro
                    block = base[d, b, fo].astype(BF) if 0 <= b <= 2 else jnp.zeros((64, 128), BF)
                    w[top : top + 64, ri * 128 : ri * 128 + 128] = block


def column(ref):
    n = ref.shape[1]
    wide = ref[...]
    if n < 128:
        wide = jnp.concatenate([wide, jnp.zeros((1, 128 - n), F32)], axis=1)
    return jnp.broadcast_to(wide, (128, 128)).T[0:n]


def scales_of(fw):
    both = column(fw)
    return jnp.where(lax.axis_index("tm") == 0, both[0:8], both[8:16])


def put_strips(lane, row, tile, left, right):
    turned = pltpu.roll(tile, 3 * row + 3, 1)
    left = jnp.where((lane >= 3 * row + 3) & (lane < 3 * row + 6), turned, left)
    right = jnp.where((lane >= 3 * row) & (lane < 3 * row + 3), turned, right)
    return left, right


def slab_kernel(xt, slab):
    slab[...] = xt[:, pl.ds(pl.multiple_of(256 - 224 * lax.axis_index("tm"), 32), 32), :]


def slab_of(xt):
    return pl.pallas_call(
        slab_kernel,
        in_specs=[VMEM],
        out_specs=VMEM,
        out_shape=struct((32, 32, 128)),
        compiler_params=params(),
        cost_estimate=cost(1e3, 1e3),
        name="slab",
    )(xt)


def halo_kernel(e_rows, o_rows, after, out):
    at = pl.ds(pl.multiple_of(224 * (1 - lax.axis_index("tm")), 32), 32)
    out[0:3] = e_rows[:, at, :]
    out[3:6] = o_rows[:, at, :]


def halo(e_rows, o_rows, after):
    return pl.pallas_call(
        halo_kernel,
        in_specs=[VMEM, VMEM, ANY],
        out_specs=VMEM,
        out_shape=struct((6, 32, 128)),
        compiler_params=params(),
        cost_estimate=cost(1e10, 1e5),
        name="halo",
    )(e_rows, o_rows, after)


def strip_pack_kernel(left0, right0, e_rows, o_rows, slab, corner, after, left, right, e_send, o_send, edge):
    lane = lanes_of((16, 128))
    even = lax.axis_index("row") % 2 == 0
    even_col = lax.axis_index("col") % 2 == 0
    e_at = jnp.where(even, 3, 0)
    for k, (source, at) in enumerate(((e_rows, e_at), (o_rows, 3 - e_at))):
        edge[pl.ds(at, 3), 0:256] = source[...]
        edge[pl.ds(at, 3), 256:288] = corner[3 * k : 3 * k + 3]

    def add_edges(at, pair):
        for k in range(6):
            pair = put_strips(lane, k if k < 3 else 32 + k, edge[k, at, :], *pair)
        first, last = pltpu.roll(pair[0], 125, 1), pair[1]
        left[at, :] = first
        right[at, :] = last
        e_send[at, :] = jnp.where(even_col, last, first)
        o_send[at, :] = jnp.where(even_col, first, last)

    for s in range(16):
        at = slice(s * 16, s * 16 + 16)
        add_edges(at, (left0[at, :], right0[at, :]))

    for s in range(2):
        at = slice(s * 16, s * 16 + 16)
        pair = jnp.zeros((16, 128), BF), jnp.zeros((16, 128), BF)
        for row in range(32):
            pair = put_strips(lane, row + 3, slab[row, at, :], *pair)
        add_edges(slice(256 + s * 16, 272 + s * 16), pair)


def strip_pack(*args):
    return pl.pallas_call(
        strip_pack_kernel,
        in_specs=[VMEM] * 6 + [ANY],
        out_specs=[VMEM] * 4,
        out_shape=[struct((288, 128))] * 4,
        scratch_shapes=[pltpu.VMEM((6, 288, 128), BF)],
        compiler_params=params(),
        cost_estimate=cost(1e8, 1e6),
        name="strip_pack",
    )(*args)


def unit(acc, w, wide_bias, read, scales):
    rows = [read(k) for k in range(6)]
    rhs = jnp.concatenate(
        [jnp.concatenate([rows[ri], rows[ri + 2]], axis=1) for ri in range(4)], axis=0
    )
    y = dot(w[...], rhs)
    acc = list(acc)
    for fo in range(2):
        for half in range(2):
            cols = slice(128 * half, 128 * half + 128)
            part = [y[d * 256 + fo * 128 : d * 256 + fo * 128 + 128, cols] for d in range(3)]
            z = part[1] + pltpu.roll(part[0], 1, 1) + pltpu.roll(part[2], 127, 1) + wide_bias
            acc[half] = acc[half] + jnp.maximum(z, 0.0) * scales[fo]
    return acc


def blank():
    return [jnp.zeros((128, 128), F32) for _ in range(2)]


def store_quad(ref, base, acc):
    for half in range(2):
        for ro in range(2):
            ref[base + 2 * half + ro] = acc[half][ro * 64 : ro * 64 + 64].astype(ref.dtype)


def load_quad(ref, base):
    return [
        jnp.concatenate([ref[base + 2 * half], ref[base + 2 * half + 1]], axis=0) for half in range(2)
    ]


def interior_kernel(xt, kt, b0, fw, out, left, right, w):
    t = lax.axis_index("tm")
    bias = column(b0)
    wide_bias = jnp.concatenate([bias, bias], axis=0)
    scale = scales_of(fw)
    scale = jnp.where(t == 0, scale[0:6], scale[2:8])
    fill_w(taps(kt), w)

    for n in range(7):
        base = 4 * n
        acc = blank()
        for k in range(3):
            at = pl.ds(pl.multiple_of(64 * (k + t), 64), 128)
            scales = [scale[2 * k + fo : 2 * k + fo + 1] for fo in range(2)]
            acc = unit(acc, w, wide_bias, lambda r: xt[base + 1 + r, at, :], scales)
        store_quad(out, base, acc)

    lane = lanes_of((16, 128))

    @pl.loop(0, 16)
    def _(s):
        at = pl.ds(pl.multiple_of(s * 16, 16), 16)
        source = pl.ds(pl.multiple_of(s * 16 + 32, 16), 16)
        pair = jnp.zeros((16, 128), BF), jnp.zeros((16, 128), BF)
        for row in range(32):
            pair = put_strips(lane, row + 3, xt[row, source, :], *pair)
        left[at, :], right[at, :] = pair


def interior(xt, kt, b0, fw):
    return pl.pallas_call(
        interior_kernel,
        in_specs=[VMEM] * 4,
        out_specs=[VMEM] * 3,
        out_shape=[struct((28, 64, 128), F32), struct((256, 128)), struct((256, 128))],
        scratch_shapes=[pltpu.VMEM((768, 512), BF)],
        compiler_params=params(),
        cost_estimate=cost(1e3, 1e3),
        name="interior",
    )(xt, kt, b0, fw)


def edges_kernel(xt, e_rows, o_rows, after, kt, b0, fw, out, edge, w):
    t = lax.axis_index("tm")
    bias = column(b0)
    wide_bias = jnp.concatenate([bias, bias], axis=0)
    scale = scales_of(fw)
    scale = jnp.where(t == 0, scale[0:6], scale[2:8])
    fill_w(taps(kt), w)
    even = lax.axis_index("row") % 2 == 0
    for low in range(2):
        edge[low, :, 0:32] = jnp.zeros((6, 32, 128), BF)
        edge[low, :, 288:320] = jnp.zeros((6, 32, 128), BF)
        edge[low, 3 - 3 * low : 6 - 3 * low, 32:288] = xt[29 * low : 29 * low + 3, 32:288]
        first, second = (o_rows, e_rows) if low == 0 else (e_rows, o_rows)
        edge[low, 3 * low : 3 * low + 3, 32:288] = jnp.where(even, first[...], second[...])
    for low in range(2):
        acc = blank()
        for k in range(3):
            at = pl.ds(pl.multiple_of(64 * (k + t), 64), 128)
            scales = [scale[2 * k + fo : 2 * k + fo + 1] for fo in range(2)]
            acc = unit(acc, w, wide_bias, lambda r: edge[low, r, at, :], scales)
        store_quad(out, 4 * low, acc)


def edge_quads(xt, e_rows, o_rows, after, kt, b0, fw):
    return pl.pallas_call(
        edges_kernel,
        in_specs=[VMEM] * 3 + [ANY] + [VMEM] * 3,
        out_specs=VMEM,
        out_shape=struct((8, 64, 128), F32),
        scratch_shapes=[pltpu.VMEM((2, 6, 320, 128), BF), pltpu.VMEM((768, 512), BF)],
        compiler_params=params(),
        cost_estimate=cost(6 * 768 * 512 * 256 * 2, 2e6),
        name="edge_quads",
    )(xt, e_rows, o_rows, after, kt, b0, fw)


def rest_kernel(own, xt, inner, slab, kt, b0, fw, *refs):
    if own:
        outer, e_rows, o_rows, corner, out, far, edge, w = refs
        quads = 3
    else:
        out, mid, w = refs
        quads = 4
    t = lax.axis_index("tm")
    start = 16 * t if own else 12 * (1 - t)
    bias = column(b0)
    wide_bias = jnp.concatenate([bias, bias], axis=0)
    fill_w({key: jnp.where(t == 1, pltpu.roll(value, 96, 1), value) for key, value in taps(kt).items()}, w)
    own_at = pl.ds(pl.multiple_of(192 - 160 * t, 32), 96)
    scale = scales_of(fw)
    scale = jnp.where(t == 0, scale[6:8], scale[0:2])
    scales = [scale[fo : fo + 1] for fo in range(2)]

    for i in range(quads):
        at = start + 4 * i

        def read(r):
            return jnp.concatenate([xt[at + 1 + r, own_at, :], slab[at + 1 + r]], axis=0)

        acc = unit(load_quad(inner, at), w, wide_bias, read, scales)
        store_quad(out, 4 * i + 4 * (1 - t) if own else 4 * i, acc)
        if not own and i in (0, 3):

            @pl.when(t == i // 3)
            def _():
                store_quad(mid, 0, acc)

    if own:
        halo_at = pl.ds(pl.multiple_of(160 - 160 * t, 32), 96)
        for far_edge in range(2):
            low = 1 - t if far_edge else t
            from_e = (lax.axis_index("row") + low) % 2 == 1
            rows = edge.at[far_edge]
            rows[pl.ds(3 - 3 * low, 3), 0:96] = xt[pl.ds(29 * low, 3), own_at]
            rows[pl.ds(3 - 3 * low, 3), 96:128] = slab[pl.ds(29 * low, 3)]
            rows[pl.ds(3 * low, 3), 0:96] = jnp.where(from_e, e_rows[:, halo_at, :], o_rows[:, halo_at, :])
            rows[pl.ds(3 * low, 3), 96:128] = jnp.where(from_e, corner[0:3], corner[3:6])
            acc = unit(load_quad(outer, 4 * low), w, wide_bias, lambda r: rows[r], scales)
            if far_edge:
                store_quad(far, 0, acc)
            else:
                store_quad(out, 12 * t, acc)


def rest(own, *args):
    scratch = [pltpu.VMEM((768, 512), BF)]
    if own:
        out_shape = [struct((16, 64, 128), F32), struct((4, 64, 128))]
        scratch = [pltpu.VMEM((2, 6, 128, 128), BF)] + scratch
    else:
        out_shape = [struct((16, 64, 128)), struct((4, 64, 128), F32)]
    return pl.pallas_call(
        functools.partial(rest_kernel, own),
        in_specs=[VMEM] * len(args),
        out_specs=[VMEM] * len(out_shape),
        out_shape=out_shape,
        scratch_shapes=scratch,
        compiler_params=params(),
        cost_estimate=cost(1e6, 1e6),
        name="rest_own" if own else "rest_partner",
    )(*args)


def strip_temporal_kernel(own_l, own_r, e_col, o_col, kt, b0, fw, out, send, windows, ws):
    t = lax.axis_index("tm")
    even = lax.axis_index("col") % 2 == 0
    lane = lanes_of((16, 128))
    third = lane % 3
    bias = column(b0)
    for (d, b, fo), value in taps(kt).items():
        ws[fo * 64 : fo * 64 + 64, (b * 3 + d) * 128 : (b * 3 + d) * 128 + 128] = value.astype(BF)

    windows[:, pl.ds(pl.multiple_of(288 * t, 32), 32), :] = jnp.zeros((9, 32, 256), BF)

    def fill(s, at):
        src = slice(s * 16, s * 16 + 16)
        dst = pl.ds(at if isinstance(at, int) else pl.multiple_of(at, 16), 16)
        ol, orr, ne, no = own_l[src, :], own_r[src, :], e_col[src, :], o_col[src, :]
        nl, nr = jnp.where(even, no, ne), jnp.where(even, ne, no)
        for b in range(3):
            for d in range(3):
                lo = pltpu.roll(nl, (128 - (3 * b + d)) % 128, 1)
                if d > 0:
                    lo = jnp.where(third < 3 - d, lo, pltpu.roll(ol, (128 - (3 * b + d - 3)) % 128, 1))
                hi = pltpu.roll(nr, (128 - (3 * b + d - 2)) % 128, 1)
                if d < 2:
                    hi = jnp.where(third < 2 - d, pltpu.roll(orr, 128 - (3 * b + d + 1), 1), hi)
                windows[b * 3 + d, dst, 0:128] = lo
                windows[b * 3 + d, dst, 128:256] = hi

    for s in range(18):
        fill(s, 32 + 16 * s if s < 16 else 288 * (1 - t) + (s - 16) * 16)

    wide_bias = jnp.concatenate([bias, bias], axis=1)
    both = scales_of(fw)
    both = jnp.concatenate([both, both], axis=1)
    scale = [both[k : k + 1] for k in range(8)]
    acc = jnp.zeros((64, 256), F32)
    for g in range(4):
        rhs = jnp.concatenate([windows[k, 64 * g : 64 * g + 128, :] for k in range(9)], axis=0)
        y = dot(ws[...], rhs)
        for fo in range(2):
            acc = acc + jnp.maximum(y[fo * 64 : fo * 64 + 64] + wide_bias, 0.0) * scale[2 * g + fo]
    for side in range(2):
        out[side] = acc[:, side * 128 : side * 128 + 128]
        send[side] = acc[:, side * 128 : side * 128 + 128].astype(BF)


def spatial_weights_kernel(k1, b1, k2, b2, after, w1, w2, c1, c2):
    w1[...] = k1[...].reshape(576, 128).astype(F32).T.astype(BF)
    for k in range(9):
        w2[:, k * 128 : k * 128 + 128] = k2[k // 3, k % 3]
    c1[...] = column(b1)
    c2[...] = column(b2)


def spatial_weights(*args):
    return pl.pallas_call(
        spatial_weights_kernel,
        in_specs=[VMEM] * 4 + [ANY],
        out_specs=[VMEM] * 4,
        out_shape=[struct((128, 576)), struct((128, 1152)), struct((128, 128), F32), struct((128, 128), F32)],
        compiler_params=params(),
        cost_estimate=cost(1e3, 1e3),
        name="spatial_weights",
    )(*args)


def strip_temporal(*args):
    return pl.pallas_call(
        strip_temporal_kernel,
        in_specs=[VMEM] * 7,
        out_specs=[VMEM] * 2,
        out_shape=[struct((2, 64, 128), F32), struct((2, 64, 128))],
        scratch_shapes=[pltpu.VMEM((9, 320, 256), BF), pltpu.VMEM((128, 1152), BF)],
        compiler_params=params(),
        cost_estimate=cost(1e6, 1e6),
        name="strip_temporal",
    )(*args)


def spatial_kernel(grid_rows, main, mid, partner, strips, partner_far, partner_strips, w1_ref, w2, c1, c2, out, own, theirs, c3, h3, ms):
    t = lax.axis_index("tm")
    row = lax.axis_index("row")
    col = lax.axis_index("col")
    first_col = col == 0
    last_col = col == lax.axis_size("col") - 1
    top = row * 32 + t * 16
    lane = lanes_of((64, 128))
    depth = lane // 3
    third = lane % 3

    own[pl.ds(4 * t, 16)] = main[...]
    own[pl.ds(16 - 16 * t, 4)] = mid[...]
    theirs[pl.ds(4 - 4 * t, 16)] = partner[...]
    theirs[pl.ds(16 * t, 4)] = partner_far[...]
    w1 = w1_ref[...]

    def in_grid(g):
        return (g >= 0) & (g < grid_rows)

    edges = []
    for side in range(2):
        total = strips[side] + partner_strips[side].astype(F32)
        total = pltpu.roll(total, (128 - 48 * t) % 128, 1)
        off = (third < 2) & first_col if side == 0 else (third > 0) & last_col
        keep = in_grid(top + depth - 2) & jnp.logical_not(off)
        edges.append(jnp.where(keep, total, 0.0).astype(BF))

    for r in range(20):
        value = (own[r] + theirs[r].astype(F32)).astype(BF)
        value = jnp.where(lane == 0, pltpu.roll(edges[0], (126 - 3 * r) % 128, 1), value)
        value = jnp.where(lane == 127, pltpu.roll(edges[1], 127 - 3 * r, 1), value)
        value = jnp.where(in_grid(top + r - 2), value, jnp.zeros_like(value))
        c3[r, 0:64] = jnp.where(lane == 0, pltpu.roll(edges[0], 127 - 3 * r, 1), pltpu.roll(value, 1, 1))
        c3[r, 64:128] = value
        c3[r, 128:192] = jnp.where(
            lane == 127, pltpu.roll(edges[1], 126 - 3 * r, 1), pltpu.roll(value, 127, 1)
        )

    bias1, bias2 = c1[...], c2[...]
    wide_b1 = jnp.concatenate([bias1, bias1], axis=1)
    wide_b2 = jnp.concatenate([bias2, bias2], axis=1)

    rhs = jnp.concatenate(
        [
            jnp.concatenate([pltpu.roll(edges[side], (128 - 3 * b - d) % 128, 1) for side in range(2)], axis=1)
            for b in range(3)
            for d in range(3)
        ],
        axis=0,
    )
    y = jnp.maximum(dot(w1, rhs) + wide_b1, 0.0)
    lane2 = lanes_of((128, 128))
    kept = in_grid(top + lane2 // 3 - 1)
    hs_l = jnp.where(kept & jnp.logical_not(first_col), y[:, :128], 0.0).astype(BF)
    hs_r = jnp.where(kept & jnp.logical_not(last_col), y[:, 128:], 0.0).astype(BF)

    for h in range(0, 18, 2):
        rhs = jnp.concatenate(
            [jnp.concatenate([c3[h + b], c3[h + 1 + b]], axis=1) for b in range(3)], axis=0
        )
        y = jnp.maximum(dot(w1, rhs) + wide_b1, 0.0)
        for at in range(h, h + 2):
            value = y[:, (at - h) * 128 : (at - h) * 128 + 128].astype(BF)
            value = jnp.where(in_grid(top + at - 1), value, jnp.zeros_like(value))
            h3[at, 0:128] = jnp.where(
                lane2 == 0, pltpu.roll(hs_l, (128 - 3 * at) % 128, 1), pltpu.roll(value, 1, 1)
            )
            h3[at, 128:256] = value
            h3[at, 256:384] = jnp.where(
                lane2 == 127, pltpu.roll(hs_r, 127 - 3 * at, 1), pltpu.roll(value, 127, 1)
            )

    for r in range(0, 16, 2):
        rhs = jnp.concatenate(
            [jnp.concatenate([h3[r + b], h3[r + 1 + b]], axis=1) for b in range(3)], axis=0
        )
        y = jnp.maximum(dot(w2[...], rhs) + wide_b2, 0.0).astype(BF)
        ms[r] = y[:, :128]
        ms[r + 1] = y[:, 128:]

    perm = swap16()
    for pair in range(4):
        halves = [ms[:, (2 * pair + k) * 16 : (2 * pair + k) * 16 + 16, :].reshape(256, 128) for k in range(2)]
        y = dot(perm, jnp.concatenate(halves, axis=1)).astype(BF)
        for k in range(2):
            q = (2 * pair + k) * 16
            out[q : q + 16] = y[:, k * 128 : k * 128 + 128].reshape(16, 16, 128)


def spatial(grid_rows, *args):
    return pl.pallas_call(
        functools.partial(spatial_kernel, grid_rows),
        in_specs=[VMEM] * 10,
        out_specs=VMEM,
        out_shape=struct((128, 16, 128)),
        scratch_shapes=[
            pltpu.VMEM((20, 64, 128), F32),
            pltpu.VMEM((20, 64, 128), BF),
            pltpu.VMEM((20, 192, 128), BF),
            pltpu.VMEM((18, 384, 128), BF),
            pltpu.VMEM((16, 128, 128), BF),
        ],
        compiler_params=params(),
        cost_estimate=cost(1.2e9, 3e6),
        name="spatial",
    )(*args)


def swaps(count, odd):
    return [pair for i in range(odd, count - 1, 2) for pair in ((i, i + 1), (i + 1, i))]


def shards(sweeps, kt, b0, fw, k1, b1, k2, b2):
    rows = lax.axis_size("row")
    cols = lax.axis_size("col")
    both = [(0, 1), (1, 0)]
    kt = jnp.transpose(kt, (2, 3, 4, 1, 0))
    k1 = jnp.transpose(k1, (2, 3, 1, 0))
    k2 = jnp.transpose(k2, (2, 3, 0, 1))
    b0, fw, b1, b2 = (value.reshape(1, -1) for value in (b0, fw, b1, b2))

    xt, e_rows, o_rows = pack(sweeps)
    e_rows = lax.ppermute(e_rows, "row", swaps(rows, 0))
    o_rows = lax.ppermute(o_rows, "row", swaps(rows, 1))
    slab = lax.ppermute(slab_of(xt), "tm", both)
    inner, left0, right0 = interior(xt, kt, b0, fw)
    field = (xt, inner, slab, kt, b0, fw)
    for_partner, mid = rest(False, *field)
    partner = lax.ppermute(for_partner, "tm", both)

    corner = halo(e_rows, o_rows, mid)
    outer = edge_quads(xt, e_rows, o_rows, corner, kt, b0, fw)
    corner = lax.ppermute(corner, "tm", both)
    left, right, e_col, o_col = strip_pack(left0, right0, e_rows, o_rows, slab, corner, outer)
    o_col = lax.ppermute(o_col, "col", swaps(cols, 1))
    e_col = lax.ppermute(e_col, "col", swaps(cols, 0))
    main, far = rest(True, *field, outer, e_rows, o_rows, corner)
    far = lax.ppermute(far, "tm", both)
    strips, strips_send = strip_temporal(left, right, e_col, o_col, kt, b0, fw)
    w1, w2, c1, c2 = spatial_weights(k1, b1, k2, b2, strips)
    strips_recv = lax.ppermute(strips_send, "tm", both)
    return spatial(rows * 32, main, mid, partner, strips, far, strips_recv, w1, w2, c1, c2)


def solution(mesh):
    placed = (P(None, "tm", "row", "col"), P(), P(), P(), P(), P(), P(), P())
    return jax.shard_map(
        shards, mesh=mesh, in_specs=placed, out_specs=P(None, ("row", "tm"), "col"), check_vma=False
    )
```

```python
import functools

import jax
import jax.numpy as jnp
from jax import lax
from jax.experimental import pallas as pl
from jax.experimental.pallas import tpu as pltpu
from jax.sharding import PartitionSpec as P

BF = jnp.bfloat16
F32 = jnp.float32
ANY = pl.BlockSpec(memory_space=pl.ANY)
VMEM = pl.BlockSpec(memory_space=pltpu.VMEM)


def params(mib=14):
    return pltpu.CompilerParams(vmem_limit_bytes=mib * 1024 * 1024)


def cost(flops, nbytes):
    return pl.CostEstimate(flops=int(flops), bytes_accessed=int(nbytes), transcendentals=0)


def struct(shape, dtype=BF):
    return jax.ShapeDtypeStruct(shape, dtype)


def dot(a, b):
    return jnp.dot(a, b, preferred_element_type=F32)


def lanes_of(shape):
    return lax.broadcasted_iota(jnp.int32, shape, len(shape) - 1)


def swap16():
    row = lax.broadcasted_iota(jnp.int32, (256, 256), 0)
    col = lax.broadcasted_iota(jnp.int32, (256, 256), 1)
    return jnp.where(col == (row % 16) * 16 + row // 16, 1.0, 0.0).astype(BF)


def pack_kernel(x, xt, e_rows, o_rows):
    even = lax.axis_index("row") % 2 == 0
    perm = swap16()
    xt[:, 0:32, :] = jnp.zeros((32, 32, 128), BF)
    xt[:, 288:320, :] = jnp.zeros((32, 32, 128), BF)
    for f in range(8):
        for cb in range(2):
            halves = [
                x[cb * 16 : cb * 16 + 16, f, rb * 16 : rb * 16 + 16, :].reshape(256, 128) for rb in range(2)
            ]
            y = dot(perm, jnp.concatenate(halves, axis=1)).astype(BF)
            at = 32 + 32 * f + 16 * cb
            for rb in range(2):
                xt[rb * 16 : rb * 16 + 16, at : at + 16, :] = y[:, rb * 128 : rb * 128 + 128].reshape(16, 16, 128)
    e_start = jnp.where(even, 29, 0)
    e_rows[...] = xt[pl.ds(e_start, 3), 32:288]
    o_rows[...] = xt[pl.ds(29 - e_start, 3), 32:288]


def pack(sweeps):
    return pl.pallas_call(
        pack_kernel,
        in_specs=[VMEM],
        out_specs=[VMEM] * 3,
        out_shape=[
            struct((32, 320, 128)),
            struct((3, 256, 128)),
            struct((3, 256, 128)),
        ],
        compiler_params=params(),
        cost_estimate=cost(6e9, 4.6e6),
        name="pack",
    )(sweeps)


def taps(kt):
    base = {}
    for d in range(3):
        for b in range(3):
            rows = [kt[a, b, d].astype(F32) for a in range(3)] + [jnp.zeros((32, 64), F32)]
            value = jnp.concatenate(rows, axis=0).T
            base[d, b, 0] = value
            base[d, b, 1] = pltpu.roll(value, 32, 1)
    return base


def fill_w(base, w):
    for d in range(3):
        for fo in range(2):
            for ro in range(2):
                top = d * 256 + fo * 128 + ro * 64
                for ri in range(4):
                    b = ri - ro
                    block = base[d, b, fo].astype(BF) if 0 <= b <= 2 else jnp.zeros((64, 128), BF)
                    w[top : top + 64, ri * 128 : ri * 128 + 128] = block


def column(ref):
    n = ref.shape[1]
    wide = ref[...]
    if n < 128:
        wide = jnp.concatenate([wide, jnp.zeros((1, 128 - n), F32)], axis=1)
    return jnp.broadcast_to(wide, (128, 128)).T[0:n]


def scales_of(fw):
    both = column(fw)
    return jnp.where(lax.axis_index("tm") == 0, both[0:8], both[8:16])


def put_strips(lane, row, tile, left, right):
    turned = pltpu.roll(tile, 3 * row + 3, 1)
    left = jnp.where((lane >= 3 * row + 3) & (lane < 3 * row + 6), turned, left)
    right = jnp.where((lane >= 3 * row) & (lane < 3 * row + 3), turned, right)
    return left, right


def slab_kernel(xt, slab):
    slab[...] = xt[:, pl.ds(pl.multiple_of(256 - 224 * lax.axis_index("tm"), 32), 32), :]


def slab_of(xt):
    return pl.pallas_call(
        slab_kernel,
        in_specs=[VMEM],
        out_specs=VMEM,
        out_shape=struct((32, 32, 128)),
        compiler_params=params(),
        cost_estimate=cost(1e3, 1e3),
        name="slab",
    )(xt)


def halo_kernel(e_rows, o_rows, after, out):
    at = pl.ds(pl.multiple_of(224 * (1 - lax.axis_index("tm")), 32), 32)
    out[0:3] = e_rows[:, at, :]
    out[3:6] = o_rows[:, at, :]


def halo(e_rows, o_rows, after):
    return pl.pallas_call(
        halo_kernel,
        in_specs=[VMEM, VMEM, ANY],
        out_specs=VMEM,
        out_shape=struct((6, 32, 128)),
        compiler_params=params(),
        cost_estimate=cost(1e10, 1e5),
        name="halo",
    )(e_rows, o_rows, after)


def strip_pack_kernel(left0, right0, e_rows, o_rows, slab, corner, after, for_partner, left, right, e_send, o_send, send, edge):
    send[...] = for_partner[...]
    lane = lanes_of((16, 128))
    even = lax.axis_index("row") % 2 == 0
    even_col = lax.axis_index("col") % 2 == 0
    e_at = jnp.where(even, 3, 0)
    for k, (source, at) in enumerate(((e_rows, e_at), (o_rows, 3 - e_at))):
        edge[pl.ds(at, 3), 0:256] = source[...]
        edge[pl.ds(at, 3), 256:288] = corner[3 * k : 3 * k + 3]

    def add_edges(at, pair):
        for k in range(6):
            pair = put_strips(lane, k if k < 3 else 32 + k, edge[k, at, :], *pair)
        first, last = pltpu.roll(pair[0], 125, 1), pair[1]
        left[at, :] = first
        right[at, :] = last
        e_send[at, :] = jnp.where(even_col, last, first)
        o_send[at, :] = jnp.where(even_col, first, last)

    for s in range(16):
        at = slice(s * 16, s * 16 + 16)
        add_edges(at, (left0[at, :], right0[at, :]))

    for s in range(2):
        at = slice(s * 16, s * 16 + 16)
        pair = jnp.zeros((16, 128), BF), jnp.zeros((16, 128), BF)
        for row in range(32):
            pair = put_strips(lane, row + 3, slab[row, at, :], *pair)
        add_edges(slice(256 + s * 16, 272 + s * 16), pair)


def strip_pack(*args):
    return pl.pallas_call(
        strip_pack_kernel,
        in_specs=[VMEM] * 6 + [ANY, VMEM],
        out_specs=[VMEM] * 5,
        out_shape=[struct((288, 128))] * 4 + [struct((16, 64, 128))],
        scratch_shapes=[pltpu.VMEM((6, 288, 128), BF)],
        compiler_params=params(),
        cost_estimate=cost(1e8, 1e6),
        name="strip_pack",
    )(*args)


def unit(acc, w, wide_bias, read, scales):
    rows = [read(k) for k in range(6)]
    rhs = jnp.concatenate(
        [jnp.concatenate([rows[ri], rows[ri + 2]], axis=1) for ri in range(4)], axis=0
    )
    y = dot(w[...], rhs)
    acc = list(acc)
    for fo in range(2):
        for half in range(2):
            cols = slice(128 * half, 128 * half + 128)
            part = [y[d * 256 + fo * 128 : d * 256 + fo * 128 + 128, cols] for d in range(3)]
            z = part[1] + pltpu.roll(part[0], 1, 1) + pltpu.roll(part[2], 127, 1) + wide_bias
            acc[half] = acc[half] + jnp.maximum(z, 0.0) * scales[fo]
    return acc


def blank():
    return [jnp.zeros((128, 128), F32) for _ in range(2)]


def store_quad(ref, base, acc):
    for half in range(2):
        for ro in range(2):
            ref[base + 2 * half + ro] = acc[half][ro * 64 : ro * 64 + 64].astype(ref.dtype)


def load_quad(ref, base):
    return [
        jnp.concatenate([ref[base + 2 * half], ref[base + 2 * half + 1]], axis=0) for half in range(2)
    ]


def interior_kernel(xt, kt, b0, fw, out, left, right, w):
    t = lax.axis_index("tm")
    bias = column(b0)
    wide_bias = jnp.concatenate([bias, bias], axis=0)
    scale = scales_of(fw)
    scale = jnp.where(t == 0, scale[0:6], scale[2:8])
    fill_w(taps(kt), w)

    for n in range(7):
        base = 4 * n
        acc = blank()
        for k in range(3):
            at = pl.ds(pl.multiple_of(64 * (k + t), 64), 128)
            scales = [scale[2 * k + fo : 2 * k + fo + 1] for fo in range(2)]
            acc = unit(acc, w, wide_bias, lambda r: xt[base + 1 + r, at, :], scales)
        store_quad(out, base, acc)

    lane = lanes_of((16, 128))

    @pl.loop(0, 16)
    def _(s):
        at = pl.ds(pl.multiple_of(s * 16, 16), 16)
        source = pl.ds(pl.multiple_of(s * 16 + 32, 16), 16)
        pair = jnp.zeros((16, 128), BF), jnp.zeros((16, 128), BF)
        for row in range(32):
            pair = put_strips(lane, row + 3, xt[row, source, :], *pair)
        left[at, :], right[at, :] = pair


def interior(xt, kt, b0, fw):
    return pl.pallas_call(
        interior_kernel,
        in_specs=[VMEM] * 4,
        out_specs=[VMEM] * 3,
        out_shape=[struct((28, 64, 128), F32), struct((256, 128)), struct((256, 128))],
        scratch_shapes=[pltpu.VMEM((768, 512), BF)],
        compiler_params=params(),
        cost_estimate=cost(1e3, 1e3),
        name="interior",
    )(xt, kt, b0, fw)


def edges_kernel(xt, e_rows, o_rows, after, kt, b0, fw, out, edge, w):
    t = lax.axis_index("tm")
    bias = column(b0)
    wide_bias = jnp.concatenate([bias, bias], axis=0)
    scale = scales_of(fw)
    scale = jnp.where(t == 0, scale[0:6], scale[2:8])
    fill_w(taps(kt), w)
    even = lax.axis_index("row") % 2 == 0
    for low in range(2):
        edge[low, :, 0:32] = jnp.zeros((6, 32, 128), BF)
        edge[low, :, 288:320] = jnp.zeros((6, 32, 128), BF)
        edge[low, 3 - 3 * low : 6 - 3 * low, 32:288] = xt[29 * low : 29 * low + 3, 32:288]
        first, second = (o_rows, e_rows) if low == 0 else (e_rows, o_rows)
        edge[low, 3 * low : 3 * low + 3, 32:288] = jnp.where(even, first[...], second[...])
    for low in range(2):
        acc = blank()
        for k in range(3):
            at = pl.ds(pl.multiple_of(64 * (k + t), 64), 128)
            scales = [scale[2 * k + fo : 2 * k + fo + 1] for fo in range(2)]
            acc = unit(acc, w, wide_bias, lambda r: edge[low, r, at, :], scales)
        store_quad(out, 4 * low, acc)


def edge_quads(xt, e_rows, o_rows, after, kt, b0, fw):
    return pl.pallas_call(
        edges_kernel,
        in_specs=[VMEM] * 3 + [ANY] + [VMEM] * 3,
        out_specs=VMEM,
        out_shape=struct((8, 64, 128), F32),
        scratch_shapes=[pltpu.VMEM((2, 6, 320, 128), BF), pltpu.VMEM((768, 512), BF)],
        compiler_params=params(),
        cost_estimate=cost(6 * 768 * 512 * 256 * 2, 2e6),
        name="edge_quads",
    )(xt, e_rows, o_rows, after, kt, b0, fw)


def rest_kernel(own, xt, inner, slab, kt, b0, fw, *refs):
    if own:
        outer, e_rows, o_rows, corner, out, far, edge, w = refs
        quads = 3
    else:
        out, mid, w = refs
        quads = 4
    t = lax.axis_index("tm")
    start = 16 * t if own else 12 * (1 - t)
    bias = column(b0)
    wide_bias = jnp.concatenate([bias, bias], axis=0)
    fill_w({key: jnp.where(t == 1, pltpu.roll(value, 96, 1), value) for key, value in taps(kt).items()}, w)
    own_at = pl.ds(pl.multiple_of(192 - 160 * t, 32), 96)
    scale = scales_of(fw)
    scale = jnp.where(t == 0, scale[6:8], scale[0:2])
    scales = [scale[fo : fo + 1] for fo in range(2)]

    for i in range(quads):
        at = start + 4 * i

        def read(r):
            return jnp.concatenate([xt[at + 1 + r, own_at, :], slab[at + 1 + r]], axis=0)

        acc = unit(load_quad(inner, at), w, wide_bias, read, scales)
        store_quad(out, 4 * i + 4 * (1 - t) if own else 4 * i, acc)
        if not own and i in (0, 3):

            @pl.when(t == i // 3)
            def _():
                store_quad(mid, 0, acc)

    if own:
        halo_at = pl.ds(pl.multiple_of(160 - 160 * t, 32), 96)
        for far_edge in range(2):
            low = 1 - t if far_edge else t
            from_e = (lax.axis_index("row") + low) % 2 == 1
            rows = edge.at[far_edge]
            rows[pl.ds(3 - 3 * low, 3), 0:96] = xt[pl.ds(29 * low, 3), own_at]
            rows[pl.ds(3 - 3 * low, 3), 96:128] = slab[pl.ds(29 * low, 3)]
            rows[pl.ds(3 * low, 3), 0:96] = jnp.where(from_e, e_rows[:, halo_at, :], o_rows[:, halo_at, :])
            rows[pl.ds(3 * low, 3), 96:128] = jnp.where(from_e, corner[0:3], corner[3:6])
            acc = unit(load_quad(outer, 4 * low), w, wide_bias, lambda r: rows[r], scales)
            if far_edge:
                store_quad(far, 0, acc)
            else:
                store_quad(out, 12 * t, acc)


def rest(own, *args):
    scratch = [pltpu.VMEM((768, 512), BF)]
    if own:
        out_shape = [struct((16, 64, 128), F32), struct((4, 64, 128))]
        scratch = [pltpu.VMEM((2, 6, 128, 128), BF)] + scratch
    else:
        out_shape = [struct((16, 64, 128)), struct((4, 64, 128), F32)]
    return pl.pallas_call(
        functools.partial(rest_kernel, own),
        in_specs=[VMEM] * len(args),
        out_specs=[VMEM] * len(out_shape),
        out_shape=out_shape,
        scratch_shapes=scratch,
        compiler_params=params(),
        cost_estimate=cost(1e6, 1e6),
        name="rest_own" if own else "rest_partner",
    )(*args)


def strip_temporal_kernel(own_l, own_r, e_col, o_col, kt, b0, fw, out, send, windows, ws):
    t = lax.axis_index("tm")
    even = lax.axis_index("col") % 2 == 0
    lane = lanes_of((16, 128))
    third = lane % 3
    bias = column(b0)
    for (d, b, fo), value in taps(kt).items():
        ws[fo * 64 : fo * 64 + 64, (b * 3 + d) * 128 : (b * 3 + d) * 128 + 128] = value.astype(BF)

    windows[:, pl.ds(pl.multiple_of(288 * t, 32), 32), :] = jnp.zeros((9, 32, 256), BF)

    def fill(s, at):
        src = slice(s * 16, s * 16 + 16)
        dst = pl.ds(at if isinstance(at, int) else pl.multiple_of(at, 16), 16)
        ol, orr, ne, no = own_l[src, :], own_r[src, :], e_col[src, :], o_col[src, :]
        nl, nr = jnp.where(even, no, ne), jnp.where(even, ne, no)
        for b in range(3):
            for d in range(3):
                lo = pltpu.roll(nl, (128 - (3 * b + d)) % 128, 1)
                if d > 0:
                    lo = jnp.where(third < 3 - d, lo, pltpu.roll(ol, (128 - (3 * b + d - 3)) % 128, 1))
                hi = pltpu.roll(nr, (128 - (3 * b + d - 2)) % 128, 1)
                if d < 2:
                    hi = jnp.where(third < 2 - d, pltpu.roll(orr, 128 - (3 * b + d + 1), 1), hi)
                windows[b * 3 + d, dst, 0:128] = lo
                windows[b * 3 + d, dst, 128:256] = hi

    for s in range(18):
        fill(s, 32 + 16 * s if s < 16 else 288 * (1 - t) + (s - 16) * 16)

    wide_bias = jnp.concatenate([bias, bias], axis=1)
    both = scales_of(fw)
    both = jnp.concatenate([both, both], axis=1)
    scale = [both[k : k + 1] for k in range(8)]
    acc = jnp.zeros((64, 256), F32)
    for g in range(4):
        rhs = jnp.concatenate([windows[k, 64 * g : 64 * g + 128, :] for k in range(9)], axis=0)
        y = dot(ws[...], rhs)
        for fo in range(2):
            acc = acc + jnp.maximum(y[fo * 64 : fo * 64 + 64] + wide_bias, 0.0) * scale[2 * g + fo]
    for side in range(2):
        out[side] = acc[:, side * 128 : side * 128 + 128]
        send[side] = acc[:, side * 128 : side * 128 + 128].astype(BF)


def spatial_weights_kernel(k1, b1, k2, b2, after, w1, w2, c1, c2):
    w1[...] = k1[...].reshape(576, 128).astype(F32).T.astype(BF)
    for k in range(9):
        w2[:, k * 128 : k * 128 + 128] = k2[k // 3, k % 3]
    c1[...] = column(b1)
    c2[...] = column(b2)


def spatial_weights(*args):
    return pl.pallas_call(
        spatial_weights_kernel,
        in_specs=[VMEM] * 4 + [ANY],
        out_specs=[VMEM] * 4,
        out_shape=[struct((128, 576)), struct((128, 1152)), struct((128, 128), F32), struct((128, 128), F32)],
        compiler_params=params(),
        cost_estimate=cost(1e3, 1e3),
        name="spatial_weights",
    )(*args)


def strip_temporal(*args):
    return pl.pallas_call(
        strip_temporal_kernel,
        in_specs=[VMEM] * 7,
        out_specs=[VMEM] * 2,
        out_shape=[struct((2, 64, 128), F32), struct((2, 64, 128))],
        scratch_shapes=[pltpu.VMEM((9, 320, 256), BF), pltpu.VMEM((128, 1152), BF)],
        compiler_params=params(),
        cost_estimate=cost(1e6, 1e6),
        name="strip_temporal",
    )(*args)


def spatial_kernel(grid_rows, main, mid, partner, strips, partner_far, partner_strips, w1_ref, w2, c1, c2, out, own, theirs, c3, h3, ms):
    t = lax.axis_index("tm")
    row = lax.axis_index("row")
    col = lax.axis_index("col")
    first_col = col == 0
    last_col = col == lax.axis_size("col") - 1
    top = row * 32 + t * 16
    lane = lanes_of((64, 128))
    depth = lane // 3
    third = lane % 3

    own[pl.ds(4 * t, 16)] = main[...]
    own[pl.ds(16 - 16 * t, 4)] = mid[...]
    theirs[pl.ds(4 - 4 * t, 16)] = partner[...]
    theirs[pl.ds(16 * t, 4)] = partner_far[...]
    w1 = w1_ref[...]

    def in_grid(g):
        return (g >= 0) & (g < grid_rows)

    edges = []
    for side in range(2):
        total = strips[side] + partner_strips[side].astype(F32)
        total = pltpu.roll(total, (128 - 48 * t) % 128, 1)
        off = (third < 2) & first_col if side == 0 else (third > 0) & last_col
        keep = in_grid(top + depth - 2) & jnp.logical_not(off)
        edges.append(jnp.where(keep, total, 0.0).astype(BF))

    for r in range(20):
        value = (own[r] + theirs[r].astype(F32)).astype(BF)
        value = jnp.where(lane == 0, pltpu.roll(edges[0], (126 - 3 * r) % 128, 1), value)
        value = jnp.where(lane == 127, pltpu.roll(edges[1], 127 - 3 * r, 1), value)
        value = jnp.where(in_grid(top + r - 2), value, jnp.zeros_like(value))
        c3[r, 0:64] = jnp.where(lane == 0, pltpu.roll(edges[0], 127 - 3 * r, 1), pltpu.roll(value, 1, 1))
        c3[r, 64:128] = value
        c3[r, 128:192] = jnp.where(
            lane == 127, pltpu.roll(edges[1], 126 - 3 * r, 1), pltpu.roll(value, 127, 1)
        )

    bias1, bias2 = c1[...], c2[...]
    wide_b1 = jnp.concatenate([bias1, bias1], axis=1)
    wide_b2 = jnp.concatenate([bias2, bias2], axis=1)

    rhs = jnp.concatenate(
        [
            jnp.concatenate([pltpu.roll(edges[side], (128 - 3 * b - d) % 128, 1) for side in range(2)], axis=1)
            for b in range(3)
            for d in range(3)
        ],
        axis=0,
    )
    y = jnp.maximum(dot(w1, rhs) + wide_b1, 0.0)
    lane2 = lanes_of((128, 128))
    kept = in_grid(top + lane2 // 3 - 1)
    hs_l = jnp.where(kept & jnp.logical_not(first_col), y[:, :128], 0.0).astype(BF)
    hs_r = jnp.where(kept & jnp.logical_not(last_col), y[:, 128:], 0.0).astype(BF)

    for h in range(0, 18, 2):
        rhs = jnp.concatenate(
            [jnp.concatenate([c3[h + b], c3[h + 1 + b]], axis=1) for b in range(3)], axis=0
        )
        y = jnp.maximum(dot(w1, rhs) + wide_b1, 0.0)
        for at in range(h, h + 2):
            value = y[:, (at - h) * 128 : (at - h) * 128 + 128].astype(BF)
            value = jnp.where(in_grid(top + at - 1), value, jnp.zeros_like(value))
            h3[at, 0:128] = jnp.where(
                lane2 == 0, pltpu.roll(hs_l, (128 - 3 * at) % 128, 1), pltpu.roll(value, 1, 1)
            )
            h3[at, 128:256] = value
            h3[at, 256:384] = jnp.where(
                lane2 == 127, pltpu.roll(hs_r, 127 - 3 * at, 1), pltpu.roll(value, 127, 1)
            )

    for r in range(0, 16, 2):
        rhs = jnp.concatenate(
            [jnp.concatenate([h3[r + b], h3[r + 1 + b]], axis=1) for b in range(3)], axis=0
        )
        y = jnp.maximum(dot(w2[...], rhs) + wide_b2, 0.0).astype(BF)
        ms[r] = y[:, :128]
        ms[r + 1] = y[:, 128:]

    perm = swap16()
    for pair in range(4):
        halves = [ms[:, (2 * pair + k) * 16 : (2 * pair + k) * 16 + 16, :].reshape(256, 128) for k in range(2)]
        y = dot(perm, jnp.concatenate(halves, axis=1)).astype(BF)
        for k in range(2):
            q = (2 * pair + k) * 16
            out[q : q + 16] = y[:, k * 128 : k * 128 + 128].reshape(16, 16, 128)


def spatial(grid_rows, *args):
    return pl.pallas_call(
        functools.partial(spatial_kernel, grid_rows),
        in_specs=[VMEM] * 10,
        out_specs=VMEM,
        out_shape=struct((128, 16, 128)),
        scratch_shapes=[
            pltpu.VMEM((20, 64, 128), F32),
            pltpu.VMEM((20, 64, 128), BF),
            pltpu.VMEM((20, 192, 128), BF),
            pltpu.VMEM((18, 384, 128), BF),
            pltpu.VMEM((16, 128, 128), BF),
        ],
        compiler_params=params(),
        cost_estimate=cost(1.2e9, 3e6),
        name="spatial",
    )(*args)


def swaps(count, odd):
    return [pair for i in range(odd, count - 1, 2) for pair in ((i, i + 1), (i + 1, i))]


def shards(sweeps, kt, b0, fw, k1, b1, k2, b2):
    rows = lax.axis_size("row")
    cols = lax.axis_size("col")
    both = [(0, 1), (1, 0)]
    kt = jnp.transpose(kt, (2, 3, 4, 1, 0))
    k1 = jnp.transpose(k1, (2, 3, 1, 0))
    k2 = jnp.transpose(k2, (2, 3, 0, 1))
    b0, fw, b1, b2 = (value.reshape(1, -1) for value in (b0, fw, b1, b2))

    xt, e_rows, o_rows = pack(sweeps)
    e_rows = lax.ppermute(e_rows, "row", swaps(rows, 0))
    o_rows = lax.ppermute(o_rows, "row", swaps(rows, 1))
    slab = lax.ppermute(slab_of(xt), "tm", both)
    inner, left0, right0 = interior(xt, kt, b0, fw)
    field = (xt, inner, slab, kt, b0, fw)
    for_partner, mid = rest(False, *field)
    corner = halo(e_rows, o_rows, mid)
    outer = edge_quads(xt, e_rows, o_rows, corner, kt, b0, fw)
    corner = lax.ppermute(corner, "tm", both)
    packed = strip_pack(left0, right0, e_rows, o_rows, slab, corner, outer, for_partner)
    left, right, e_col, o_col, for_partner = packed
    partner = lax.ppermute(for_partner, "tm", both)
    o_col = lax.ppermute(o_col, "col", swaps(cols, 1))
    e_col = lax.ppermute(e_col, "col", swaps(cols, 0))
    main, far = rest(True, *field, outer, e_rows, o_rows, corner)
    far = lax.ppermute(far, "tm", both)
    strips, strips_send = strip_temporal(left, right, e_col, o_col, kt, b0, fw)
    w1, w2, c1, c2 = spatial_weights(k1, b1, k2, b2, strips)
    strips_recv = lax.ppermute(strips_send, "tm", both)
    return spatial(rows * 32, main, mid, partner, strips, far, strips_recv, w1, w2, c1, c2)


def solution(mesh):
    placed = (P(None, "tm", "row", "col"), P(), P(), P(), P(), P(), P(), P())
    return jax.shard_map(
        shards, mesh=mesh, in_specs=placed, out_specs=P(None, ("row", "tm"), "col"), check_vma=False
    )
```

```python
import functools

import jax
import jax.numpy as jnp
from jax import lax
from jax.experimental import pallas as pl
from jax.experimental.pallas import tpu as pltpu
from jax.sharding import PartitionSpec as P

BF = jnp.bfloat16
F32 = jnp.float32
ANY = pl.BlockSpec(memory_space=pl.ANY)
VMEM = pl.BlockSpec(memory_space=pltpu.VMEM)


def params(mib=14):
    return pltpu.CompilerParams(vmem_limit_bytes=mib * 1024 * 1024)


def cost(flops, nbytes):
    return pl.CostEstimate(flops=int(flops), bytes_accessed=int(nbytes), transcendentals=0)


def struct(shape, dtype=BF):
    return jax.ShapeDtypeStruct(shape, dtype)


def dot(a, b):
    return jnp.dot(a, b, preferred_element_type=F32)


def lanes_of(shape):
    return lax.broadcasted_iota(jnp.int32, shape, len(shape) - 1)


def swap16():
    row = lax.broadcasted_iota(jnp.int32, (256, 256), 0)
    col = lax.broadcasted_iota(jnp.int32, (256, 256), 1)
    return jnp.where(col == (row % 16) * 16 + row // 16, 1.0, 0.0).astype(BF)


def pack_kernel(x, xt, e_rows, o_rows):
    even = lax.axis_index("row") % 2 == 0
    perm = swap16()
    xt[:, 0:32, :] = jnp.zeros((32, 32, 128), BF)
    xt[:, 288:320, :] = jnp.zeros((32, 32, 128), BF)
    for f in range(8):
        for cb in range(2):
            halves = [
                x[cb * 16 : cb * 16 + 16, f, rb * 16 : rb * 16 + 16, :].reshape(256, 128) for rb in range(2)
            ]
            y = dot(perm, jnp.concatenate(halves, axis=1)).astype(BF)
            at = 32 + 32 * f + 16 * cb
            for rb in range(2):
                xt[rb * 16 : rb * 16 + 16, at : at + 16, :] = y[:, rb * 128 : rb * 128 + 128].reshape(16, 16, 128)
    e_start = jnp.where(even, 29, 0)
    e_rows[...] = xt[pl.ds(e_start, 3), 32:288]
    o_rows[...] = xt[pl.ds(29 - e_start, 3), 32:288]


def pack(sweeps):
    return pl.pallas_call(
        pack_kernel,
        in_specs=[VMEM],
        out_specs=[VMEM] * 3,
        out_shape=[
            struct((32, 320, 128)),
            struct((3, 256, 128)),
            struct((3, 256, 128)),
        ],
        compiler_params=params(),
        cost_estimate=cost(6e9, 4.6e6),
        name="pack",
    )(sweeps)


def taps(kt):
    base = {}
    for d in range(3):
        for b in range(3):
            rows = [kt[a, b, d].astype(F32) for a in range(3)] + [jnp.zeros((32, 64), F32)]
            value = jnp.concatenate(rows, axis=0).T
            base[d, b, 0] = value
            base[d, b, 1] = pltpu.roll(value, 32, 1)
    return base


def fill_w(base, w):
    for d in range(3):
        for fo in range(2):
            for ro in range(2):
                top = d * 256 + fo * 128 + ro * 64
                for ri in range(4):
                    b = ri - ro
                    block = base[d, b, fo].astype(BF) if 0 <= b <= 2 else jnp.zeros((64, 128), BF)
                    w[top : top + 64, ri * 128 : ri * 128 + 128] = block


def column(ref):
    n = ref.shape[1]
    wide = ref[...]
    if n < 128:
        wide = jnp.concatenate([wide, jnp.zeros((1, 128 - n), F32)], axis=1)
    return jnp.broadcast_to(wide, (128, 128)).T[0:n]


def scales_of(fw):
    both = column(fw)
    return jnp.where(lax.axis_index("tm") == 0, both[0:8], both[8:16])


def put_strips(lane, row, tile, left, right):
    turned = pltpu.roll(tile, 3 * row + 3, 1)
    left = jnp.where((lane >= 3 * row + 3) & (lane < 3 * row + 6), turned, left)
    right = jnp.where((lane >= 3 * row) & (lane < 3 * row + 3), turned, right)
    return left, right


def slab_kernel(xt, slab):
    slab[...] = xt[:, pl.ds(pl.multiple_of(256 - 224 * lax.axis_index("tm"), 32), 32), :]


def slab_of(xt):
    return pl.pallas_call(
        slab_kernel,
        in_specs=[VMEM],
        out_specs=VMEM,
        out_shape=struct((32, 32, 128)),
        compiler_params=params(),
        cost_estimate=cost(1e3, 1e3),
        name="slab",
    )(xt)


def halo_kernel(e_rows, o_rows, after, out):
    at = pl.ds(pl.multiple_of(224 * (1 - lax.axis_index("tm")), 32), 32)
    out[0:3] = e_rows[:, at, :]
    out[3:6] = o_rows[:, at, :]


def halo(e_rows, o_rows, after):
    return pl.pallas_call(
        halo_kernel,
        in_specs=[VMEM, VMEM, ANY],
        out_specs=VMEM,
        out_shape=struct((6, 32, 128)),
        compiler_params=params(),
        cost_estimate=cost(1e10, 1e5),
        name="halo",
    )(e_rows, o_rows, after)


def strip_pack_kernel(left0, right0, e_rows, o_rows, slab, corner, after, for_partner, left, right, e_send, o_send, send, edge):
    send[...] = for_partner[...]
    lane = lanes_of((16, 128))
    even = lax.axis_index("row") % 2 == 0
    even_col = lax.axis_index("col") % 2 == 0
    e_at = jnp.where(even, 3, 0)
    for k, (source, at) in enumerate(((e_rows, e_at), (o_rows, 3 - e_at))):
        edge[pl.ds(at, 3), 0:256] = source[...]
        edge[pl.ds(at, 3), 256:288] = corner[3 * k : 3 * k + 3]

    def add_edges(at, pair):
        for k in range(6):
            pair = put_strips(lane, k if k < 3 else 32 + k, edge[k, at, :], *pair)
        first, last = pltpu.roll(pair[0], 125, 1), pair[1]
        left[at, :] = first
        right[at, :] = last
        e_send[at, :] = jnp.where(even_col, last, first)
        o_send[at, :] = jnp.where(even_col, first, last)

    for s in range(16):
        at = slice(s * 16, s * 16 + 16)
        add_edges(at, (left0[at, :], right0[at, :]))

    for s in range(2):
        at = slice(s * 16, s * 16 + 16)
        pair = jnp.zeros((16, 128), BF), jnp.zeros((16, 128), BF)
        for row in range(32):
            pair = put_strips(lane, row + 3, slab[row, at, :], *pair)
        add_edges(slice(256 + s * 16, 272 + s * 16), pair)


def strip_pack(*args):
    return pl.pallas_call(
        strip_pack_kernel,
        in_specs=[VMEM] * 6 + [ANY, VMEM],
        out_specs=[VMEM] * 5,
        out_shape=[struct((288, 128))] * 4 + [struct((16, 64, 128))],
        scratch_shapes=[pltpu.VMEM((6, 288, 128), BF)],
        compiler_params=params(),
        cost_estimate=cost(1e8, 1e6),
        name="strip_pack",
    )(*args)


def unit(acc, w, wide_bias, read, scales):
    rows = [read(k) for k in range(6)]
    rhs = jnp.concatenate(
        [jnp.concatenate([rows[ri], rows[ri + 2]], axis=1) for ri in range(4)], axis=0
    )
    y = dot(w[...], rhs)
    acc = list(acc)
    for fo in range(2):
        for half in range(2):
            cols = slice(128 * half, 128 * half + 128)
            part = [y[d * 256 + fo * 128 : d * 256 + fo * 128 + 128, cols] for d in range(3)]
            z = part[1] + pltpu.roll(part[0], 1, 1) + pltpu.roll(part[2], 127, 1) + wide_bias
            acc[half] = acc[half] + jnp.maximum(z, 0.0) * scales[fo]
    return acc


def blank():
    return [jnp.zeros((128, 128), F32) for _ in range(2)]


def store_quad(ref, base, acc):
    for half in range(2):
        for ro in range(2):
            ref[base + 2 * half + ro] = acc[half][ro * 64 : ro * 64 + 64].astype(ref.dtype)


def load_quad(ref, base):
    return [
        jnp.concatenate([ref[base + 2 * half], ref[base + 2 * half + 1]], axis=0) for half in range(2)
    ]


def interior_kernel(xt, kt, b0, fw, out, left, right, w):
    t = lax.axis_index("tm")
    bias = column(b0)
    wide_bias = jnp.concatenate([bias, bias], axis=0)
    scale = scales_of(fw)
    scale = jnp.where(t == 0, scale[0:6], scale[2:8])
    fill_w(taps(kt), w)

    for n in range(7):
        base = 4 * n
        acc = blank()
        for k in range(3):
            at = pl.ds(pl.multiple_of(64 * (k + t), 64), 128)
            scales = [scale[2 * k + fo : 2 * k + fo + 1] for fo in range(2)]
            acc = unit(acc, w, wide_bias, lambda r: xt[base + 1 + r, at, :], scales)
        store_quad(out, base, acc)

    lane = lanes_of((16, 128))

    @pl.loop(0, 16)
    def _(s):
        at = pl.ds(pl.multiple_of(s * 16, 16), 16)
        source = pl.ds(pl.multiple_of(s * 16 + 32, 16), 16)
        pair = jnp.zeros((16, 128), BF), jnp.zeros((16, 128), BF)
        for row in range(32):
            pair = put_strips(lane, row + 3, xt[row, source, :], *pair)
        left[at, :], right[at, :] = pair


def interior(xt, kt, b0, fw):
    return pl.pallas_call(
        interior_kernel,
        in_specs=[VMEM] * 4,
        out_specs=[VMEM] * 3,
        out_shape=[struct((28, 64, 128), F32), struct((256, 128)), struct((256, 128))],
        scratch_shapes=[pltpu.VMEM((768, 512), BF)],
        compiler_params=params(),
        cost_estimate=cost(1e3, 1e3),
        name="interior",
    )(xt, kt, b0, fw)


def edges_kernel(xt, e_rows, o_rows, after, kt, b0, fw, out, edge, w):
    t = lax.axis_index("tm")
    bias = column(b0)
    wide_bias = jnp.concatenate([bias, bias], axis=0)
    scale = scales_of(fw)
    scale = jnp.where(t == 0, scale[0:6], scale[2:8])
    fill_w(taps(kt), w)
    even = lax.axis_index("row") % 2 == 0
    for low in range(2):
        edge[low, :, 0:32] = jnp.zeros((6, 32, 128), BF)
        edge[low, :, 288:320] = jnp.zeros((6, 32, 128), BF)
        edge[low, 3 - 3 * low : 6 - 3 * low, 32:288] = xt[29 * low : 29 * low + 3, 32:288]
        first, second = (o_rows, e_rows) if low == 0 else (e_rows, o_rows)
        edge[low, 3 * low : 3 * low + 3, 32:288] = jnp.where(even, first[...], second[...])
    for low in range(2):
        acc = blank()
        for k in range(3):
            at = pl.ds(pl.multiple_of(64 * (k + t), 64), 128)
            scales = [scale[2 * k + fo : 2 * k + fo + 1] for fo in range(2)]
            acc = unit(acc, w, wide_bias, lambda r: edge[low, r, at, :], scales)
        store_quad(out, 4 * low, acc)


def edge_quads(xt, e_rows, o_rows, after, kt, b0, fw):
    return pl.pallas_call(
        edges_kernel,
        in_specs=[VMEM] * 3 + [ANY] + [VMEM] * 3,
        out_specs=VMEM,
        out_shape=struct((8, 64, 128), F32),
        scratch_shapes=[pltpu.VMEM((2, 6, 320, 128), BF), pltpu.VMEM((768, 512), BF)],
        compiler_params=params(),
        cost_estimate=cost(6 * 768 * 512 * 256 * 2, 2e6),
        name="edge_quads",
    )(xt, e_rows, o_rows, after, kt, b0, fw)


def rest_kernel(own, xt, inner, slab, kt, b0, fw, *refs):
    if own:
        outer, e_rows, o_rows, corner, out, far, edge, w = refs
        quads = 3
    else:
        out, mid, ws, c0, fws, w = refs
        quads = 4
    t = lax.axis_index("tm")
    start = 16 * t if own else 12 * (1 - t)
    bias = column(b0)
    wide_bias = jnp.concatenate([bias, bias], axis=0)
    base = taps(kt)
    fill_w({key: jnp.where(t == 1, pltpu.roll(value, 96, 1), value) for key, value in base.items()}, w)
    own_at = pl.ds(pl.multiple_of(192 - 160 * t, 32), 96)
    scale = scales_of(fw)
    if not own:
        c0[...] = bias
        fws[...] = scale
        for (d, b, fo), value in base.items():
            ws[fo * 64 : fo * 64 + 64, (b * 3 + d) * 128 : (b * 3 + d) * 128 + 128] = value.astype(BF)
    scale = jnp.where(t == 0, scale[6:8], scale[0:2])
    scales = [scale[fo : fo + 1] for fo in range(2)]

    for i in range(quads):
        at = start + 4 * i

        def read(r):
            return jnp.concatenate([xt[at + 1 + r, own_at, :], slab[at + 1 + r]], axis=0)

        acc = unit(load_quad(inner, at), w, wide_bias, read, scales)
        store_quad(out, 4 * i + 4 * (1 - t) if own else 4 * i, acc)
        if not own and i in (0, 3):

            @pl.when(t == i // 3)
            def _():
                store_quad(mid, 0, acc)

    if own:
        halo_at = pl.ds(pl.multiple_of(160 - 160 * t, 32), 96)
        for far_edge in range(2):
            low = 1 - t if far_edge else t
            from_e = (lax.axis_index("row") + low) % 2 == 1
            rows = edge.at[far_edge]
            rows[pl.ds(3 - 3 * low, 3), 0:96] = xt[pl.ds(29 * low, 3), own_at]
            rows[pl.ds(3 - 3 * low, 3), 96:128] = slab[pl.ds(29 * low, 3)]
            rows[pl.ds(3 * low, 3), 0:96] = jnp.where(from_e, e_rows[:, halo_at, :], o_rows[:, halo_at, :])
            rows[pl.ds(3 * low, 3), 96:128] = jnp.where(from_e, corner[0:3], corner[3:6])
            acc = unit(load_quad(outer, 4 * low), w, wide_bias, lambda r: rows[r], scales)
            if far_edge:
                store_quad(far, 0, acc)
            else:
                store_quad(out, 12 * t, acc)


def rest(own, *args):
    scratch = [pltpu.VMEM((768, 512), BF)]
    if own:
        out_shape = [struct((16, 64, 128), F32), struct((4, 64, 128))]
        scratch = [pltpu.VMEM((2, 6, 128, 128), BF)] + scratch
    else:
        out_shape = [struct((16, 64, 128)), struct((4, 64, 128), F32)]
        out_shape += [struct((128, 1152)), struct((64, 128), F32), struct((8, 128), F32)]
    return pl.pallas_call(
        functools.partial(rest_kernel, own),
        in_specs=[VMEM] * len(args),
        out_specs=[VMEM] * len(out_shape),
        out_shape=out_shape,
        scratch_shapes=scratch,
        compiler_params=params(),
        cost_estimate=cost(1e6, 1e6),
        name="rest_own" if own else "rest_partner",
    )(*args)


def strip_temporal_kernel(own_l, own_r, e_col, o_col, ws, c0, fws, out, send, windows):
    t = lax.axis_index("tm")
    even = lax.axis_index("col") % 2 == 0
    lane = lanes_of((16, 128))
    third = lane % 3
    bias = c0[...]

    windows[:, pl.ds(pl.multiple_of(288 * t, 32), 32), :] = jnp.zeros((9, 32, 256), BF)

    def fill(s, at):
        src = slice(s * 16, s * 16 + 16)
        dst = pl.ds(at if isinstance(at, int) else pl.multiple_of(at, 16), 16)
        ol, orr, ne, no = own_l[src, :], own_r[src, :], e_col[src, :], o_col[src, :]
        nl, nr = jnp.where(even, no, ne), jnp.where(even, ne, no)
        ol, nr = pltpu.roll(ol, 3, 1), pltpu.roll(nr, 3, 1)
        for d in range(3):
            lo = nl if d == 0 else jnp.where(third >= d, nl, ol)
            hi = nr if d == 2 else jnp.where(third >= d + 1, orr, nr)
            for b in range(3):
                turn = 3 * b + d
                windows[b * 3 + d, dst, 0:128] = pltpu.roll(lo, (128 - turn) % 128, 1)
                windows[b * 3 + d, dst, 128:256] = pltpu.roll(hi, 127 - turn, 1)

    for s in range(18):
        fill(s, 32 + 16 * s if s < 16 else 288 * (1 - t) + (s - 16) * 16)

    wide_bias = jnp.concatenate([bias, bias], axis=1)
    both = jnp.concatenate([fws[...], fws[...]], axis=1)
    scale = [both[k : k + 1] for k in range(8)]
    acc = jnp.zeros((64, 256), F32)
    for g in range(4):
        rhs = jnp.concatenate([windows[k, 64 * g : 64 * g + 128, :] for k in range(9)], axis=0)
        y = dot(ws[...], rhs)
        for fo in range(2):
            acc = acc + jnp.maximum(y[fo * 64 : fo * 64 + 64] + wide_bias, 0.0) * scale[2 * g + fo]
    for side in range(2):
        out[side] = acc[:, side * 128 : side * 128 + 128]
        send[side] = acc[:, side * 128 : side * 128 + 128].astype(BF)


def spatial_weights_kernel(k1, b1, k2, b2, after, w1, w2, c1, c2, perm):
    perm[...] = swap16()
    w1[...] = k1[...].reshape(576, 128).astype(F32).T.astype(BF)
    for k in range(9):
        w2[:, k * 128 : k * 128 + 128] = k2[k // 3, k % 3]
    c1[...] = column(b1)
    c2[...] = column(b2)


def spatial_weights(*args):
    return pl.pallas_call(
        spatial_weights_kernel,
        in_specs=[VMEM] * 4 + [ANY],
        out_specs=[VMEM] * 5,
        out_shape=[
            struct((128, 576)),
            struct((128, 1152)),
            struct((128, 128), F32),
            struct((128, 128), F32),
            struct((256, 256)),
        ],
        compiler_params=params(),
        cost_estimate=cost(1e3, 1e3),
        name="spatial_weights",
    )(*args)


def strip_temporal(*args):
    return pl.pallas_call(
        strip_temporal_kernel,
        in_specs=[VMEM] * 7,
        out_specs=[VMEM] * 2,
        out_shape=[struct((2, 64, 128), F32), struct((2, 64, 128))],
        scratch_shapes=[pltpu.VMEM((9, 320, 256), BF)],
        compiler_params=params(),
        cost_estimate=cost(1e6, 1e6),
        name="strip_temporal",
    )(*args)


def spatial_kernel(grid_rows, main, mid, partner, strips, partner_far, partner_strips, w1_ref, w2, c1, c2, perm_ref, out, own, theirs, c3, h3, ms):
    t = lax.axis_index("tm")
    row = lax.axis_index("row")
    col = lax.axis_index("col")
    first_col = col == 0
    last_col = col == lax.axis_size("col") - 1
    top = row * 32 + t * 16
    lane = lanes_of((64, 128))
    depth = lane // 3
    third = lane % 3

    own[pl.ds(4 * t, 16)] = main[...]
    own[pl.ds(16 - 16 * t, 4)] = mid[...]
    theirs[pl.ds(4 - 4 * t, 16)] = partner[...]
    theirs[pl.ds(16 * t, 4)] = partner_far[...]
    w1 = w1_ref[...]

    def in_grid(g):
        return (g >= 0) & (g < grid_rows)

    edges = []
    for side in range(2):
        total = strips[side] + partner_strips[side].astype(F32)
        total = pltpu.roll(total, (128 - 48 * t) % 128, 1)
        off = (third < 2) & first_col if side == 0 else (third > 0) & last_col
        keep = in_grid(top + depth - 2) & jnp.logical_not(off)
        edges.append(jnp.where(keep, total, 0.0).astype(BF))

    inner = jnp.where(third == 0, pltpu.roll(edges[0], 126, 1), pltpu.roll(edges[1], 127, 1))
    outer = jnp.where(third == 0, pltpu.roll(edges[0], 127, 1), pltpu.roll(edges[1], 126, 1))
    for r in range(20):
        turn = (128 - 3 * r) % 128
        value = (own[r] + theirs[r].astype(F32)).astype(BF)
        value = jnp.where((lane == 0) | (lane == 127), pltpu.roll(inner, turn, 1), value)
        value = jnp.where(in_grid(top + r - 2), value, jnp.zeros_like(value))
        beyond = pltpu.roll(outer, turn, 1)
        c3[r, 0:64] = jnp.where(lane == 0, beyond, pltpu.roll(value, 1, 1))
        c3[r, 64:128] = value
        c3[r, 128:192] = jnp.where(lane == 127, beyond, pltpu.roll(value, 127, 1))

    bias1, bias2 = c1[...], c2[...]
    wide_b1 = jnp.concatenate([bias1, bias1], axis=1)
    wide_b2 = jnp.concatenate([bias2, bias2], axis=1)

    rhs = jnp.concatenate(
        [
            jnp.concatenate([pltpu.roll(edges[side], (128 - 3 * b - d) % 128, 1) for side in range(2)], axis=1)
            for b in range(3)
            for d in range(3)
        ],
        axis=0,
    )
    y = jnp.maximum(dot(w1, rhs) + wide_b1, 0.0)
    lane2 = lanes_of((128, 128))
    kept = in_grid(top + lane2 // 3 - 1)
    hs_l = jnp.where(kept & jnp.logical_not(first_col), y[:, :128], 0.0).astype(BF)
    hs_r = jnp.where(kept & jnp.logical_not(last_col), y[:, 128:], 0.0).astype(BF)
    sides = jnp.where(lane2 % 3 == 0, hs_l, pltpu.roll(hs_r, 127, 1))

    for h in range(0, 18, 2):
        rhs = jnp.concatenate(
            [jnp.concatenate([c3[h + b], c3[h + 1 + b]], axis=1) for b in range(3)], axis=0
        )
        y = jnp.maximum(dot(w1, rhs) + wide_b1, 0.0)
        for at in range(h, h + 2):
            value = y[:, (at - h) * 128 : (at - h) * 128 + 128].astype(BF)
            value = jnp.where(in_grid(top + at - 1), value, jnp.zeros_like(value))
            beyond = pltpu.roll(sides, (128 - 3 * at) % 128, 1)
            h3[at, 0:128] = jnp.where(lane2 == 0, beyond, pltpu.roll(value, 1, 1))
            h3[at, 128:256] = value
            h3[at, 256:384] = jnp.where(lane2 == 127, beyond, pltpu.roll(value, 127, 1))

    for r in range(0, 16, 2):
        rhs = jnp.concatenate(
            [jnp.concatenate([h3[r + b], h3[r + 1 + b]], axis=1) for b in range(3)], axis=0
        )
        y = jnp.maximum(dot(w2[...], rhs) + wide_b2, 0.0).astype(BF)
        ms[r] = y[:, :128]
        ms[r + 1] = y[:, 128:]

    perm = perm_ref[...]
    for pair in range(4):
        halves = [ms[:, (2 * pair + k) * 16 : (2 * pair + k) * 16 + 16, :].reshape(256, 128) for k in range(2)]
        y = dot(perm, jnp.concatenate(halves, axis=1)).astype(BF)
        for k in range(2):
            q = (2 * pair + k) * 16
            out[q : q + 16] = y[:, k * 128 : k * 128 + 128].reshape(16, 16, 128)


def spatial(grid_rows, *args):
    return pl.pallas_call(
        functools.partial(spatial_kernel, grid_rows),
        in_specs=[VMEM] * 11,
        out_specs=VMEM,
        out_shape=struct((128, 16, 128)),
        scratch_shapes=[
            pltpu.VMEM((20, 64, 128), F32),
            pltpu.VMEM((20, 64, 128), BF),
            pltpu.VMEM((20, 192, 128), BF),
            pltpu.VMEM((18, 384, 128), BF),
            pltpu.VMEM((16, 128, 128), BF),
        ],
        compiler_params=params(),
        cost_estimate=cost(1.2e9, 3e6),
        name="spatial",
    )(*args)


def swaps(count, odd):
    return [pair for i in range(odd, count - 1, 2) for pair in ((i, i + 1), (i + 1, i))]


def shards(sweeps, kt, b0, fw, k1, b1, k2, b2):
    rows = lax.axis_size("row")
    cols = lax.axis_size("col")
    both = [(0, 1), (1, 0)]
    kt = jnp.transpose(kt, (2, 3, 4, 1, 0))
    k1 = jnp.transpose(k1, (2, 3, 1, 0))
    k2 = jnp.transpose(k2, (2, 3, 0, 1))
    b0, fw, b1, b2 = (value.reshape(1, -1) for value in (b0, fw, b1, b2))

    xt, e_rows, o_rows = pack(sweeps)
    e_rows = lax.ppermute(e_rows, "row", swaps(rows, 0))
    o_rows = lax.ppermute(o_rows, "row", swaps(rows, 1))
    slab = lax.ppermute(slab_of(xt), "tm", both)
    inner, left0, right0 = interior(xt, kt, b0, fw)
    field = (xt, inner, slab, kt, b0, fw)
    for_partner, mid, ws, c0, fws = rest(False, *field)
    corner = halo(e_rows, o_rows, mid)
    outer = edge_quads(xt, e_rows, o_rows, corner, kt, b0, fw)
    corner = lax.ppermute(corner, "tm", both)
    packed = strip_pack(left0, right0, e_rows, o_rows, slab, corner, outer, for_partner)
    left, right, e_col, o_col, for_partner = packed
    partner = lax.ppermute(for_partner, "tm", both)
    o_col = lax.ppermute(o_col, "col", swaps(cols, 1))
    e_col = lax.ppermute(e_col, "col", swaps(cols, 0))
    main, far = rest(True, *field, outer, e_rows, o_rows, corner)
    far = lax.ppermute(far, "tm", both)
    strips, strips_send = strip_temporal(left, right, e_col, o_col, ws, c0, fws)
    laid_out = spatial_weights(k1, b1, k2, b2, strips)
    strips_recv = lax.ppermute(strips_send, "tm", both)
    return spatial(rows * 32, main, mid, partner, strips, far, strips_recv, *laid_out)


def solution(mesh):
    placed = (P(None, "tm", "row", "col"), P(), P(), P(), P(), P(), P(), P())
    return jax.shard_map(
        shards, mesh=mesh, in_specs=placed, out_specs=P(None, ("row", "tm"), "col"), check_vma=False
    )
```
